256 devices in a mesh: batch: 32 (over y, x, core), tensor: 8 (over z).
Axes of the slice: x: 4, y: 4, z: 8, core: 2. Of those that a mesh axis runs over, the one named last changes fastest.
Arguments:
- normed_hidden_rows: bfloat16 [4, 512, 8192], P(None, 'batch', 'tensor'), may hold values from -6 to 6
- queries: bfloat16 [4, 512, 8192], P(None, 'batch', 'tensor'), may hold values from -6 to 6
- key_weight: bfloat16 [8192, 1024], P('tensor'), may hold values from -0.0625 to 0.0625
- value_weight: bfloat16 [8192, 1024], P('tensor'), may hold values from -0.0625 to 0.0625
- adapter_down: bfloat16 [1024, 64, 8192], P('batch', None, 'tensor'), may hold values from -0.0625 to 0.0625
- adapter_up: bfloat16 [1024, 64, 1024], P('batch', None, 'tensor'), may hold values from -0.75 to 0.75
- adapter_ids: int32 [512], P('batch'), may hold values from 0 to 1023, as said below
- owner_map: int32 [1024], replicated, may hold values from 0 to 1023, as said below
- cache_keys: bfloat16 [512, 8, 256, 128], P('batch', 'tensor'), may hold values from -6 to 6
- cache_values: bfloat16 [512, 8, 256, 128], P('batch', 'tensor'), may hold values from -6 to 6
- cache_lengths: int32 [512], P('batch'), may hold values from 2 to 256, as said below
Outputs:
- new_keys: bfloat16 [4, 512, 1024], P(None, 'batch', 'tensor')
- incoming_values: bfloat16 [4, 512, 1024], P(None, 'batch', 'tensor')
- attention: bfloat16 [4, 512, 8192], P(None, 'batch', 'tensor')
The draws below stay inside these ranges and needn't reach their ends.
Inputs may be any that keep to these rules, and one draw needn't show every extreme that they name: A permutation: adapter a is stored in row owner_map[a] of adapter_down and adapter_up, whose owner is owner_map[a] // 32. `adapter_ids`: among the 16 requests of one device at most 2 have adapters of one owner; in every draw one owner has exactly 2 requests from every device. `cache_lengths`: some request has exactly 256.
All inputs are finite; a program needn't handle non-finite values.
Results may differ from the reference program's by a relative error of at most 0.0095.
Values may be sent and summed in bfloat16 or wider, within the bound.
No kernel may reach another device: no remote copies, remote signals or barrier semaphores. Data moves between devices by JAX's collectives and lax.ppermute only.
A program may use at most 128 MiB of HBM per device.

```python
import math
import jax
import jax.numpy as jnp
from jax import lax

D = 8192
HEADS = 64
KV_HEADS = 8
HEAD_DIM = 128
RANK = 64
ADP_DEV = 32
CAP = 2
STEPS = 4
REQ_DEV = 16
CACHE = 256
OWNERS = 32
ADAPTERS = 1024
REQUESTS = 512


def storage_order(key):
    return jax.random.permutation(jax.random.fold_in(key, 101), ADAPTERS).astype(jnp.int32)


def draw_owner_map(key, part):
    return storage_order(key)


def draw_adapter_ids(key, part):
    storage = storage_order(key)
    key = jax.random.fold_in(key, 3)
    hot_owner = jax.random.randint(jax.random.fold_in(key, 1), (), 0, OWNERS)
    candidates = jnp.arange(OWNERS * CAP, dtype=jnp.int32) // CAP

    def one_block(block_key):
        ranking = jax.random.permutation(jax.random.fold_in(block_key, 1), OWNERS * CAP).astype(jnp.int32)
        ranking = ranking + jnp.where(candidates == hot_owner, 2 * OWNERS * CAP, 0).astype(jnp.int32)
        picked = jnp.argsort(-ranking)[:REQ_DEV]
        block_owners = candidates[picked]
        shuffle = jax.random.permutation(jax.random.fold_in(block_key, 2), REQ_DEV)
        return block_owners[shuffle]
    block_keys = jax.random.split(jax.random.fold_in(key, 2), OWNERS)
    owner_rows = jax.vmap(one_block)(block_keys).reshape(REQUESTS)
    local_rows = jax.random.randint(jax.random.fold_in(key, 4), (REQUESTS,), 0, ADP_DEV)
    adapter_slot_rows = owner_rows * ADP_DEV + local_rows
    inverse = jnp.argsort(storage)
    return inverse[adapter_slot_rows].astype(jnp.int32)


def draw_cache_lengths(key, part):
    key = jax.random.fold_in(key, 9)
    lengths = jax.random.randint(jax.random.fold_in(key, 1), (REQUESTS,), 2, CACHE + 1)
    longest = jax.random.randint(jax.random.fold_in(key, 2), (), 0, REQUESTS)
    return jnp.where(jnp.arange(REQUESTS) == longest, CACHE, lengths).astype(jnp.int32)


def draw_cache_keys(key, part):
    own_key = jax.random.fold_in(key, 5)
    shape = (REQUESTS, KV_HEADS, CACHE, HEAD_DIM)
    return jnp.clip(jax.random.normal(own_key, shape, jnp.float32), -6.0, 6.0).astype(jnp.bfloat16)


def draw_queries(key, part):
    own_key = jax.random.fold_in(key, 7)
    shape = (STEPS, REQUESTS, HEADS, HEAD_DIM)
    base_draw = jnp.clip(jax.random.normal(own_key, shape, jnp.float32), -6.0, 6.0)
    return base_draw.reshape(STEPS, REQUESTS, HEADS * HEAD_DIM).astype(jnp.bfloat16)


def level_of(key, dims, cuts, smallest, top_value):
    level = 1.0
    for dim, shards_of in cuts:
        heights = jax.random.uniform(jax.random.fold_in(jax.random.fold_in(key, 6), dim), (shards_of,), jnp.float32, smallest / len(cuts), top_value / len(cuts))
        level = level * jnp.repeat(jnp.exp(heights), dims[dim] // shards_of).reshape((-1,) + (1,) * (len(dims) - 1 - dim))
    return level


def normal_values(stream_key, shape, deviation, reach, cuts=(), held_as=jnp.bfloat16):
    level = level_of(stream_key, shape, cuts, -0.22, 0.18) if cuts else 1.0
    entries = jax.random.normal(stream_key, shape, jnp.float32) * deviation * level
    return jnp.minimum(jnp.maximum(entries, -reach), reach).astype(held_as)


def setup_inputs(seed: int = 0) -> dict:
    seeds = jax.random.split(jax.random.key(seed), 12)
    return {
        "normed_hidden_rows": normal_values(seeds[0], (STEPS, REQUESTS, D), 1.0, 6.0, ((1, 32), (2, 8))),
        "queries": draw_queries(jax.random.fold_in(seeds[11], 71), 0),
        "key_weight": normal_values(seeds[2], (D, KV_HEADS * HEAD_DIM), D ** -0.5, 0.0625, ((0, 8),)),
        "value_weight": normal_values(seeds[3], (D, KV_HEADS * HEAD_DIM), D ** -0.5, 0.0625, ((0, 8),)),
        "adapter_down": normal_values(seeds[4], (ADAPTERS, RANK, D), D ** -0.5, 0.0625, ((0, 32), (2, 8))),
        "adapter_up": normal_values(seeds[5], (ADAPTERS, RANK, KV_HEADS * HEAD_DIM), RANK ** -0.5, 0.75, ((0, 32), (2, 8))),
        "adapter_ids": draw_adapter_ids(jax.random.fold_in(seeds[11], 71), 0),
        "owner_map": draw_owner_map(jax.random.fold_in(seeds[11], 71), 0),
        "cache_keys": draw_cache_keys(jax.random.fold_in(seeds[11], 71), 0),
        "cache_values": normal_values(seeds[9], (REQUESTS, KV_HEADS, CACHE, HEAD_DIM), 1.0, 6.0, ((0, 32), (1, 8))),
        "cache_lengths": draw_cache_lengths(jax.random.fold_in(seeds[11], 71), 0),
    }


ADAPTER_SCALE = 0.5
MASKED = -1e+30

def reference(normed_hidden_rows, queries, key_weight, value_weight, adapter_down, adapter_up, adapter_ids, owner_map, cache_keys, cache_values, cache_lengths):
    flat_rows = normed_hidden_rows.reshape(STEPS * REQUESTS, D)
    base_keys = jnp.dot(flat_rows, key_weight, preferred_element_type=jnp.float32).reshape(STEPS, REQUESTS, KV_HEADS * HEAD_DIM)
    frozen_value_rows = jnp.dot(flat_rows, value_weight, preferred_element_type=jnp.float32).reshape(STEPS, REQUESTS, KV_HEADS * HEAD_DIM)
    adapter_slot_rows = owner_map[adapter_ids].astype(jnp.int32)

    def single_adapter(inputs):
        request_rows, row_index = inputs
        down_rows = adapter_down[row_index]
        up_rows = adapter_up[row_index]
        shrunk = jnp.dot(request_rows, down_rows.T, preferred_element_type=jnp.float32).astype(jnp.bfloat16)
        return jnp.dot(shrunk, up_rows, preferred_element_type=jnp.float32)
    adapter_correction = lax.map(single_adapter, (jnp.swapaxes(normed_hidden_rows, 0, 1), adapter_slot_rows))
    adapter_correction = jnp.swapaxes(adapter_correction, 0, 1)
    new_keys = base_keys.astype(jnp.bfloat16)
    incoming_values = (frozen_value_rows + ADAPTER_SCALE * adapter_correction).astype(jnp.bfloat16)
    group_size = HEADS // KV_HEADS
    score_scale = 1.0 / math.sqrt(HEAD_DIM)
    cache_index = jnp.arange(CACHE, dtype=jnp.int32)
    step_index = jnp.arange(STEPS, dtype=jnp.int32)
    causal = step_index[None, :] <= step_index[:, None]

    def one_request(inputs):
        query_rows, cached_keys, cached_values, fresh_keys, fresh_values, length = inputs
        query_heads = query_rows.reshape(STEPS, KV_HEADS, group_size, HEAD_DIM).astype(jnp.float32)
        fresh_key_heads = fresh_keys.reshape(STEPS, KV_HEADS, HEAD_DIM).astype(jnp.float32)
        fresh_value_heads = fresh_values.reshape(STEPS, KV_HEADS, HEAD_DIM).astype(jnp.float32)
        past_scores = jnp.einsum('skgd,kcd->skgc', query_heads, cached_keys.astype(jnp.float32)) * score_scale
        fresh_scores = jnp.einsum('skgd,tkd->skgt', query_heads, fresh_key_heads) * score_scale
        past_scores = jnp.where((cache_index < length)[None, None, None, :], past_scores, MASKED)
        fresh_scores = jnp.where(causal[:, None, None, :], fresh_scores, MASKED)
        weights = jax.nn.softmax(jnp.concatenate([past_scores, fresh_scores], axis=-1), axis=-1).astype(jnp.bfloat16)
        weights = lax.optimization_barrier(weights).astype(jnp.float32)
        mixed = jnp.einsum('skgc,kcd->skgd', weights[..., :CACHE], cached_values.astype(jnp.float32))
        mixed = mixed + jnp.einsum('skgt,tkd->skgd', weights[..., CACHE:], fresh_value_heads)
        return mixed.reshape(STEPS, HEADS * HEAD_DIM).astype(jnp.bfloat16)
    attention = lax.map(one_request, (jnp.swapaxes(queries, 0, 1), cache_keys, cache_values, jnp.swapaxes(new_keys, 0, 1), jnp.swapaxes(incoming_values, 0, 1), cache_lengths))
    attention = jnp.swapaxes(attention, 0, 1)
    return (new_keys, incoming_values, attention)
```

```python
import math

import jax
import jax.numpy as jnp
from jax import lax
from jax.experimental import pallas as pl
from jax.experimental.pallas import tpu as pltpu
from jax.sharding import PartitionSpec as P

HEADS = 64
KV_HEADS = 8
CAP = 2

ADAPTER_SCALE = 0.5
MASKED = -1e30

F32 = jnp.float32
BF16 = jnp.bfloat16
LANES = 128
VMEM = pl.BlockSpec(memory_space=pltpu.VMEM)
SMEM = pl.BlockSpec(memory_space=pltpu.SMEM)


def params(*semantics):
    return pltpu.CompilerParams(
        dimension_semantics=semantics or None, vmem_limit_bytes=16 * 1024 * 1024
    )


def iota(shape, dim):
    return lax.broadcasted_iota(jnp.int32, shape, dim)


def contract_last(a, b):
    return lax.dot_general(a, b, (((1,), (1,)), ((), ())), preferred_element_type=F32)


def pack_kernel(ids, owner_map, x, packed, slot_of_token, counts, *, per_owner, owners):
    steps, requests, cols = x.shape
    tokens = steps * requests
    slot_rows = packed.shape[0]
    for o in range(owners):
        counts[o] = 0
    token = iota((tokens, LANES), 0) % requests
    column = iota((1, tokens), 1) % requests
    slot_sub = jnp.zeros((tokens, LANES), jnp.int32)
    row_sub = jnp.zeros((tokens, LANES), jnp.int32)
    slot_lane = jnp.zeros((1, tokens), jnp.int32)
    for r in range(requests):
        storage = owner_map[ids[r]]
        owner = storage // per_owner
        rank = counts[owner]
        counts[owner] = rank + 1
        slot = owner * CAP + rank
        slot_sub = jnp.where(token == r, slot, slot_sub)
        row_sub = jnp.where(token == r, storage - owner * per_owner, row_sub)
        slot_lane = jnp.where(column == r, slot, slot_lane)
    slot_of_token[...] = slot_sub
    place = iota((slot_rows, tokens), 0)
    source = iota((slot_rows, tokens), 1)
    chosen = (place // steps == slot_lane) & (place % steps == source // requests)
    chosen = jnp.where(chosen, 1.0, 0.0).astype(BF16)
    rows = x[...].reshape(tokens, cols)
    packed[:, :cols] = jnp.dot(chosen, rows, preferred_element_type=F32).astype(BF16)
    packed[:, cols:] = jnp.dot(
        chosen, row_sub.astype(F32).astype(BF16), preferred_element_type=F32
    ).astype(BF16)


def pack(adapter_ids, owner_map, x, per_owner, owners):
    steps, requests, cols = x.shape
    slot_rows = owners * CAP * steps
    kernel = lambda *refs: pack_kernel(*refs, per_owner=per_owner, owners=owners)
    return pl.pallas_call(
        kernel,
        out_shape=(
            jax.ShapeDtypeStruct((slot_rows, cols + LANES), BF16),
            jax.ShapeDtypeStruct((steps * requests, LANES), jnp.int32),
        ),
        in_specs=[SMEM, SMEM, VMEM],
        out_specs=(VMEM, VMEM),
        scratch_shapes=[pltpu.SMEM((owners,), jnp.int32)],
        compiler_params=params(),
        name="pack",
    )(adapter_ids, owner_map, x)


def project_kernel(x, key_weight, value_weight, out):
    tokens = out.shape[1] // 2
    rows = x[...].reshape(tokens, x.shape[2])
    out[0, :tokens] = jnp.dot(rows, key_weight[...], preferred_element_type=F32).astype(BF16)
    out[0, tokens:] = jnp.dot(rows, value_weight[...], preferred_element_type=F32).astype(BF16)


def project(x, key_weight, value_weight, heads):
    steps, requests, cols = x.shape
    head_dim = key_weight.shape[1] // heads
    tokens = steps * requests
    weight = pl.BlockSpec((cols, head_dim), lambda h: (0, h))
    return pl.pallas_call(
        project_kernel,
        grid=(heads,),
        out_shape=jax.ShapeDtypeStruct((heads, 2 * tokens, head_dim), BF16),
        in_specs=[pl.BlockSpec(x.shape, lambda h: (0, 0, 0)), weight, weight],
        out_specs=pl.BlockSpec((1, 2 * tokens, head_dim), lambda h: (h, 0, 0)),
        compiler_params=params("arbitrary"),
        cost_estimate=pl.CostEstimate(
            flops=4 * tokens * cols * heads * head_dim,
            bytes_accessed=4 * cols * heads * head_dim,
            transcendentals=0,
        ),
        name="project",
    )(x, key_weight, value_weight)


def cached_kernel(lengths, q, keys, values, out, highest, total, q_rows, *, scale):
    steps, requests, cols = q.shape
    positions, head_dim = keys.shape[2], keys.shape[3]
    groups = cols // head_dim
    rows = steps * groups
    per_step = keys.shape[0]
    block = pl.program_id(0)

    @pl.when(block == 0)
    def _():
        for s in range(steps):
            for g in range(groups):
                start = (s * groups + g) * requests
                q_rows[start : start + requests] = q[
                    s, :, g * head_dim : (g + 1) * head_dim
                ].astype(F32)

    position = iota((rows, positions), 1)
    for i in range(per_step):
        r = block * per_step + i
        mine = pl.ds(r, rows, stride=requests)
        scores = contract_last(q_rows[mine, :].astype(BF16), keys[i, 0]) * scale
        scores = jnp.where(position < lengths[r], scores, MASKED)
        top = jnp.max(scores, axis=1, keepdims=True)
        weights = jnp.exp(scores - top)
        highest[mine, :] = jnp.broadcast_to(top, (rows, LANES))
        total[mine, :] = jnp.broadcast_to(jnp.sum(weights, axis=1, keepdims=True), (rows, LANES))
        out[mine, :] = jnp.dot(weights.astype(BF16), values[i, 0], preferred_element_type=F32)


def cached_attention(lengths, q, keys, values, per_step=4):
    steps, requests, cols = q.shape
    positions, head_dim = keys.shape[2], keys.shape[3]
    rows = steps * requests * (cols // head_dim)
    cache = pl.BlockSpec((per_step, 1, positions, head_dim), lambda i: (i, 0, 0, 0))
    whole = pl.BlockSpec((rows, LANES), lambda i: (0, 0))
    kernel = lambda *refs: cached_kernel(*refs, scale=1.0 / math.sqrt(head_dim))
    return pl.pallas_call(
        kernel,
        grid=(requests // per_step,),
        out_shape=(jax.ShapeDtypeStruct((rows, LANES), F32),) * 3,
        in_specs=[SMEM, pl.BlockSpec(q.shape, lambda i: (0, 0, 0)), cache, cache],
        out_specs=(whole,) * 3,
        scratch_shapes=[pltpu.VMEM((rows, head_dim), F32)],
        compiler_params=params("arbitrary"),
        cost_estimate=pl.CostEstimate(
            flops=4 * rows * positions * head_dim,
            bytes_accessed=4 * requests * positions * head_dim,
            transcendentals=rows * positions,
        ),
        name="cached",
    )(lengths, q, keys, values)


def owned(row_ids, pair, rank, lane):
    per_vector = LANES // rank
    return row_ids == (lane // rank + pair * per_vector).astype(F32)


def shrink_kernel(received, down, projected, out, total, row_ids):
    step = pl.program_id(0)
    adapters, rank, cols = down.shape
    rows = received.shape[0]
    lane = iota((rows, LANES), 1)
    pairs = adapters * rank // LANES

    @pl.when(step == 0)
    def _():
        total[...] = jnp.zeros_like(total)
        row_ids[...] = received[:, cols:].astype(F32)

    products = contract_last(received[:, :cols], down[...].reshape(adapters * rank, cols))
    kept = total[...]
    for i in range(pairs):
        mask = owned(row_ids[...], step * pairs + i, rank, lane)
        kept = kept + jnp.where(mask, products[:, i * LANES : (i + 1) * LANES], 0.0)
    total[...] = kept

    @pl.when(step == pl.num_programs(0) - 1)
    def _():
        both = kept + pltpu.roll(kept, rank, 1)
        half = rows // 2
        partial = jnp.where(lane[:half] < rank, both[:half], both[half:]).astype(BF16)
        kv_rows = projected.shape[1]
        for t in range(out.shape[0]):
            out[t, :kv_rows] = projected[t]
            out[t, kv_rows:] = partial


def shrink(received, down, projected, per_step=8):
    adapters, rank, cols = down.shape
    rows = received.shape[0]
    heads, kv_rows, head_dim = projected.shape
    fixed = lambda shape: pl.BlockSpec(shape, lambda i: (0,) * len(shape))
    out_shape = (heads, kv_rows + rows // 2, LANES)
    return pl.pallas_call(
        shrink_kernel,
        grid=(adapters // per_step,),
        out_shape=jax.ShapeDtypeStruct(out_shape, BF16),
        in_specs=[
            fixed(received.shape),
            pl.BlockSpec((per_step, rank, cols), lambda i: (i, 0, 0)),
            fixed(projected.shape),
        ],
        out_specs=fixed(out_shape),
        scratch_shapes=[pltpu.VMEM((rows, LANES), F32), pltpu.VMEM((rows, LANES), F32)],
        compiler_params=params("arbitrary"),
        cost_estimate=pl.CostEstimate(
            flops=2 * rows * adapters * rank * cols,
            bytes_accessed=2 * adapters * rank * cols,
            transcendentals=0,
        ),
        name="shrink",
    )(received, down, projected)


def expand_kernel(summands, received, up, new_keys, base_values, correction):
    sources, all_rows, lanes = summands.shape
    adapters, rank, head_dim = up.shape
    rows = received.shape[0]
    half = rows // 2
    tokens = (all_rows - half) // 2
    total = summands[0].astype(F32)
    for t in range(1, sources):
        total = total + summands[t].astype(F32)
    new_keys[...] = total[:tokens].astype(BF16)
    base_values[...] = total[tokens : 2 * tokens]
    packed = total[2 * tokens :]
    turned = pltpu.roll(packed, rank, 1)
    low = iota((half, LANES), 1) < rank
    shrunk = jnp.concatenate(
        [jnp.where(low, packed, turned), jnp.where(low, turned, packed)], axis=0
    )
    row_ids = received[:, received.shape[1] - LANES :].astype(F32)
    lane = iota((rows, LANES), 1)
    pairs = adapters * rank // LANES
    per_vector = LANES // rank
    grown = jnp.zeros((rows, head_dim), F32)
    for i in range(pairs):
        mine = jnp.where(owned(row_ids, i, rank, lane), shrunk, 0.0).astype(BF16)
        block = up[i * per_vector : (i + 1) * per_vector].reshape(LANES, head_dim)
        grown = grown + jnp.dot(mine, block, preferred_element_type=F32)
    correction[...] = grown.astype(BF16)


def expand(summands, received, up):
    sources, all_rows, _ = summands.shape
    rows = received.shape[0]
    tokens = (all_rows - rows // 2) // 2
    head_dim = up.shape[2]
    return pl.pallas_call(
        expand_kernel,
        out_shape=(
            jax.ShapeDtypeStruct((tokens, head_dim), BF16),
            jax.ShapeDtypeStruct((tokens, head_dim), F32),
            jax.ShapeDtypeStruct((rows, head_dim), BF16),
        ),
        in_specs=[VMEM] * 3,
        out_specs=(VMEM,) * 3,
        compiler_params=params(),
        name="expand",
    )(summands, received, up)


def weigh_kernel(q, new_keys, out, highest, total, weights, mixed, *, scale):
    steps, requests, cols = q.shape
    tokens, head_dim = new_keys.shape
    groups = cols // head_dim
    keys = new_keys[...]
    rows = groups * requests
    for s in range(steps):
        q_rows = jnp.concatenate(
            [q[s, :, g * head_dim : (g + 1) * head_dim] for g in range(groups)], axis=0
        )
        scores = contract_last(q_rows, keys) * scale
        row, token = iota((rows, tokens), 0), iota((rows, tokens), 1)
        seen = (token % requests == row % requests) & (token // requests <= s)
        scores = jnp.where(seen, scores, MASKED)
        part = slice(s * rows, (s + 1) * rows)
        cached_top = highest[part, :1]
        top = jnp.maximum(jnp.max(scores, axis=1, keepdims=True), cached_top)
        fresh = jnp.exp(scores - top)
        rescale = jnp.exp(cached_top - top)
        norm = 1.0 / (total[part, :1] * rescale + jnp.sum(fresh, axis=1, keepdims=True))
        weights[part, :] = (fresh * norm).astype(BF16)
        mixed[part, :] = out[part, :] * (rescale * norm)


def weigh(q, new_keys, out, highest, total):
    rows, head_dim = out.shape
    tokens = new_keys.shape[0]
    kernel = lambda *refs: weigh_kernel(*refs, scale=1.0 / math.sqrt(head_dim))
    return pl.pallas_call(
        kernel,
        out_shape=(
            jax.ShapeDtypeStruct((rows, tokens), BF16),
            jax.ShapeDtypeStruct((rows, head_dim), F32),
        ),
        in_specs=[VMEM] * 5,
        out_specs=(VMEM,) * 2,
        compiler_params=params(),
        cost_estimate=pl.CostEstimate(
            flops=4 * rows * tokens * head_dim,
            bytes_accessed=16 * rows * head_dim,
            transcendentals=rows * tokens,
        ),
        name="weigh",
    )(q, new_keys, out, highest, total)


def finish_kernel(returned, slot_of_token, base_values, weights, mixed, values_out, attention):
    steps, requests, cols = attention.shape
    tokens, head_dim = base_values.shape
    slot_rows = returned.shape[0]
    groups = cols // head_dim
    slots = jnp.concatenate([slot_of_token[...]] * (slot_rows // LANES), axis=1)
    token, place = iota((tokens, slot_rows), 0), iota((tokens, slot_rows), 1)
    chosen = (place // steps == slots) & (place % steps == token // requests)
    chosen = jnp.where(chosen, 1.0, 0.0).astype(BF16)
    correction = jnp.dot(chosen, returned[...], preferred_element_type=F32)
    values = (base_values[...] + ADAPTER_SCALE * correction).astype(BF16)
    values_out[...] = values
    rows = groups * requests
    for s in range(steps):
        part = slice(s * rows, (s + 1) * rows)
        fresh = jnp.dot(weights[part, :], values, preferred_element_type=F32)
        result = (mixed[part, :] + fresh).astype(BF16)
        for g in range(groups):
            attention[s, :, g * head_dim : (g + 1) * head_dim] = result[
                g * requests : (g + 1) * requests
            ]


def finish(returned, slot_of_token, base_values, weights, mixed, attention_shape):
    return pl.pallas_call(
        finish_kernel,
        out_shape=(
            jax.ShapeDtypeStruct(base_values.shape, BF16),
            jax.ShapeDtypeStruct(attention_shape, BF16),
        ),
        in_specs=[VMEM] * 5,
        out_specs=(VMEM,) * 2,
        compiler_params=params(),
        name="finish",
    )(returned, slot_of_token, base_values, weights, mixed)


def per_device(
    normed_hidden_rows,
    queries,
    key_weight,
    value_weight,
    adapter_down,
    adapter_up,
    adapter_ids,
    owner_map,
    cache_keys,
    cache_values,
    cache_lengths,
):
    steps, requests, _ = normed_hidden_rows.shape
    owners = lax.axis_size("batch")
    tensor_size = lax.axis_size("tensor")
    exchange = lambda a, axis: lax.all_to_all(a, axis, split_axis=0, concat_axis=0, tiled=True)

    packed, slot_of_token = pack(
        adapter_ids, owner_map, normed_hidden_rows, adapter_down.shape[0], owners
    )
    received = exchange(packed, "batch")
    projected = project(normed_hidden_rows, key_weight, value_weight, tensor_size)
    cached = cached_attention(cache_lengths, queries, cache_keys, cache_values)
    summands = exchange(shrink(received, adapter_down, projected), "tensor")
    new_keys, base_values, correction = expand(summands, received, adapter_up)
    returned = exchange(correction, "batch")
    weights, mixed = weigh(queries, new_keys, *cached)
    values, attention = finish(
        returned, slot_of_token, base_values, weights, mixed, queries.shape
    )
    shape = (steps, requests, new_keys.shape[1])
    return (new_keys.reshape(shape), values.reshape(shape), attention)


def solution(mesh):
    placed = (
        P(None, "batch", "tensor"),
        P(None, "batch", "tensor"),
        P("tensor", None),
        P("tensor", None),
        P("batch", None, "tensor"),
        P("batch", None, "tensor"),
        P("batch"),
        P(),
        P("batch", "tensor", None, None),
        P("batch", "tensor", None, None),
        P("batch"),
    )
    return jax.shard_map(
        per_device,
        mesh=mesh,
        in_specs=placed,
        out_specs=(
            P(None, "batch", "tensor"),
            P(None, "batch", "tensor"),
            P(None, "batch", "tensor"),
        ),
        check_vma=False,
    )
```

```python
import math

import jax
import jax.numpy as jnp
from jax import lax
from jax.experimental import pallas as pl
from jax.experimental.pallas import tpu as pltpu
from jax.sharding import PartitionSpec as P

HEADS = 64
KV_HEADS = 8
CAP = 2

ADAPTER_SCALE = 0.5
MASKED = -1e30

F32 = jnp.float32
BF16 = jnp.bfloat16
LANES = 128
VMEM = pl.BlockSpec(memory_space=pltpu.VMEM)
HBM = pl.BlockSpec(memory_space=pltpu.HBM)
ANY = pl.BlockSpec(memory_space=pl.ANY)
SMEM = pl.BlockSpec(memory_space=pltpu.SMEM)


def params(mebibytes=16):
    return pltpu.CompilerParams(vmem_limit_bytes=mebibytes * 1024 * 1024)


def iota(shape, dim):
    return lax.broadcasted_iota(jnp.int32, shape, dim)


def contract_last(a, b):
    return lax.dot_general(a, b, (((1,), (1,)), ((), ())), preferred_element_type=F32)


def pack_kernel(
    ids_in, map_in, x_in, packed, slot_of_token, ids, owner_map, x, counts, sems, *, per_owner
):
    copies = [
        pltpu.make_async_copy(source, target, sems.at[i])
        for i, (source, target) in enumerate(((ids_in, ids), (map_in, owner_map), (x_in, x)))
    ]
    for copy in copies:
        copy.start()
    steps, requests, cols = x.shape
    tokens = steps * requests
    slot_rows = packed.shape[0]
    for o in range(counts.shape[0]):
        counts[o] = 0
    token = iota((tokens, LANES), 0) % requests
    column = iota((1, tokens), 1) % requests
    slot_sub = jnp.zeros((tokens, LANES), jnp.int32)
    row_sub = jnp.zeros((tokens, LANES), jnp.int32)
    slot_lane = jnp.zeros((1, tokens), jnp.int32)
    copies[0].wait()
    copies[1].wait()
    for r in range(requests):
        storage = owner_map[ids[r]]
        owner = storage // per_owner
        rank = counts[owner]
        counts[owner] = rank + 1
        slot = owner * CAP + rank
        slot_sub = jnp.where(token == r, slot, slot_sub)
        row_sub = jnp.where(token == r, storage - owner * per_owner, row_sub)
        slot_lane = jnp.where(column == r, slot, slot_lane)
    slot_of_token[...] = slot_sub
    place = iota((slot_rows, tokens), 0)
    source = iota((slot_rows, tokens), 1)
    chosen = (place // steps == slot_lane) & (place % steps == source // requests)
    chosen = jnp.where(chosen, 1.0, 0.0).astype(BF16)
    packed[:, cols:] = jnp.dot(
        chosen, row_sub.astype(F32).astype(BF16), preferred_element_type=F32
    ).astype(BF16)
    copies[2].wait()
    rows = x[...].reshape(tokens, cols)
    packed[:, :cols] = jnp.dot(chosen, rows, preferred_element_type=F32).astype(BF16)


def pack(adapter_ids, owner_map, x, per_owner, owners):
    steps, requests, cols = x.shape
    slot_rows = owners * CAP * steps
    return pl.pallas_call(
        lambda *refs: pack_kernel(*refs, per_owner=per_owner),
        out_shape=(
            jax.ShapeDtypeStruct((slot_rows, cols + LANES), BF16),
            jax.ShapeDtypeStruct((steps * requests, LANES), jnp.int32),
        ),
        in_specs=[HBM, HBM, HBM],
        out_specs=(VMEM, VMEM),
        scratch_shapes=[
            pltpu.SMEM(adapter_ids.shape, jnp.int32),
            pltpu.SMEM(owner_map.shape, jnp.int32),
            pltpu.VMEM(x.shape, BF16),
            pltpu.SMEM((owners,), jnp.int32),
            pltpu.SemaphoreType.DMA((3,)),
        ],
        compiler_params=params(60),
        name="pack",
    )(adapter_ids, owner_map, x)


def project_kernel(place, x_in, key_in, value_in, kept, given, x, key_weight, value_weight, sems):
    moves = ((x_in, x), (key_in, key_weight), (value_in, value_weight))
    copies = [
        pltpu.make_async_copy(source, target, sems.at[i])
        for i, (source, target) in enumerate(moves)
    ]
    for copy in copies:
        copy.start()
    heads, tokens, head_dim = kept.shape
    copies[0].wait()
    rows = x[...].reshape(tokens, x.shape[2])
    copies[1].wait()
    keys = jnp.dot(rows, key_weight[...], preferred_element_type=F32)
    copies[2].wait()
    values = jnp.dot(rows, value_weight[...], preferred_element_type=F32)
    even = place[0] % 2 == 0
    mine = jnp.where(even, keys, values).astype(BF16)
    other = jnp.where(even, values, keys).astype(BF16)
    for h in range(heads):
        kept[h] = mine[:, h * head_dim : (h + 1) * head_dim]
        given[h] = other[:, h * head_dim : (h + 1) * head_dim]


def project(place, x, key_weight, value_weight, heads):
    steps, requests, cols = x.shape
    tokens = steps * requests
    head_dim = key_weight.shape[1] // heads
    return pl.pallas_call(
        project_kernel,
        out_shape=(jax.ShapeDtypeStruct((heads, tokens, head_dim), BF16),) * 2,
        in_specs=[SMEM] + [HBM] * 3,
        out_specs=(VMEM,) * 2,
        scratch_shapes=[pltpu.VMEM(a.shape, BF16) for a in (x, key_weight, value_weight)]
        + [pltpu.SemaphoreType.DMA((3,))],
        compiler_params=params(60),
        cost_estimate=pl.CostEstimate(
            flops=4 * tokens * cols * heads * head_dim,
            bytes_accessed=4 * cols * heads * head_dim,
            transcendentals=0,
        ),
        name="project",
    )(place, x, key_weight, value_weight)


def pair_kernel(kept, taken, out):
    out[...] = (kept[...].astype(F32) + taken[...].astype(F32)).astype(BF16)


def pair(kept, taken):
    return pl.pallas_call(
        pair_kernel,
        out_shape=jax.ShapeDtypeStruct(kept.shape, BF16),
        in_specs=[VMEM] * 2,
        out_specs=VMEM,
        compiler_params=params(),
        name="pair",
    )(kept, taken)


def cached_kernel(
    lengths, after, q_in, cache_keys, cache_values, out, norms,
    q, keys, values, q_rows, scores, weights, sems, *, scale
):
    moves = ((q_in, q), (cache_keys, keys), (cache_values, values))
    copies = [
        pltpu.make_async_copy(source, target, sems.at[i])
        for i, (source, target) in enumerate(moves)
    ]
    for copy in copies:
        copy.start()
    steps, requests, cols = q.shape
    positions, head_dim = keys.shape[2], keys.shape[3]
    groups = cols // head_dim
    rows = steps * groups
    copies[0].wait()
    for s in range(steps):
        for g in range(groups):
            start = (s * groups + g) * requests
            q_rows[start : start + requests] = q[s, :, g * head_dim : (g + 1) * head_dim].astype(
                F32
            )
    copies[1].wait()
    position = iota((rows, positions), 1)
    low = iota((rows, LANES), 1) < LANES // 2
    for r in range(requests):
        mine = pl.ds(r, rows, stride=requests)
        product = contract_last(q_rows[mine, :].astype(BF16), keys[r, 0]) * scale
        scores[r] = jnp.where(position < lengths[r], product, MASKED)
    for r in range(requests):
        mine = pl.ds(r, rows, stride=requests)
        top = jnp.max(scores[r], axis=1, keepdims=True)
        exponent = jnp.exp(scores[r] - top)
        weights[r] = exponent.astype(BF16)
        norms[mine, :] = jnp.where(low, top, jnp.sum(exponent, axis=1, keepdims=True))
    copies[2].wait()
    for r in range(requests):
        mine = pl.ds(r, rows, stride=requests)
        out[mine, :] = jnp.dot(weights[r], values[r, 0], preferred_element_type=F32)


def cached_attention(lengths, after, q, cache_keys, cache_values):
    steps, requests, cols = q.shape
    positions, head_dim = cache_keys.shape[2], cache_keys.shape[3]
    rows = steps * requests * (cols // head_dim)
    return pl.pallas_call(
        lambda *refs: cached_kernel(*refs, scale=1.0 / math.sqrt(head_dim)),
        out_shape=(jax.ShapeDtypeStruct((rows, LANES), F32),) * 2,
        in_specs=[SMEM, ANY] + [HBM] * 3,
        out_specs=(VMEM,) * 2,
        scratch_shapes=[pltpu.VMEM(a.shape, BF16) for a in (q, cache_keys, cache_values)]
        + [
            pltpu.VMEM((rows, head_dim), F32),
            pltpu.VMEM((requests, rows // requests, positions), F32),
            pltpu.VMEM((requests, rows // requests, positions), BF16),
            pltpu.SemaphoreType.DMA((3,)),
        ],
        compiler_params=params(),
        cost_estimate=pl.CostEstimate(
            flops=4 * rows * positions * head_dim,
            bytes_accessed=4 * requests * positions * head_dim,
            transcendentals=rows * positions,
        ),
        name="cached",
    )(lengths, after, q, cache_keys, cache_values)


def shrink_kernel(received, down, partials, out, ids):
    adapters, rank, cols = down.shape
    rows = received.shape[0]
    per_part = 8
    ids[...] = received[:, cols:]
    wide = jnp.concatenate([ids[...].astype(F32)] * (rows // LANES), axis=1)
    diagonal = iota((rows, rows), 0) == iota((rows, rows), 1)
    adapter = jnp.sum(jnp.where(diagonal, wide, 0.0), axis=0, keepdims=True)
    partial = jnp.zeros((rank, rows), F32)
    for first in range(0, adapters, per_part):
        block = down[first : first + per_part].reshape(per_part * rank, cols)
        products = contract_last(block, received[:, :cols])
        for i in range(per_part):
            mine = adapter == float(first + i)
            partial = jnp.where(mine, products[i * rank : (i + 1) * rank], partial)
    partial = partial.astype(BF16)
    tokens = partials.shape[1]
    for t in range(out.shape[0]):
        out[t, :tokens] = partials[t]
        for i in range(rows // LANES):
            start = tokens + i * rank
            out[t, start : start + rank] = partial[:, i * LANES : (i + 1) * LANES]


def shrink(received, down, partials):
    adapters, rank, cols = down.shape
    rows = received.shape[0]
    heads, tokens, _ = partials.shape
    return pl.pallas_call(
        shrink_kernel,
        out_shape=(
            jax.ShapeDtypeStruct((heads, tokens + rank * rows // LANES, LANES), BF16),
            jax.ShapeDtypeStruct((rows, LANES), BF16),
        ),
        in_specs=[VMEM] * 3,
        out_specs=(VMEM,) * 2,
        compiler_params=params(),
        cost_estimate=pl.CostEstimate(
            flops=2 * rows * adapters * rank * cols,
            bytes_accessed=2 * adapters * rank * cols,
            transcendentals=0,
        ),
        name="shrink",
    )(received, down, partials)


def lane_keys(row_ids, rank):
    return row_ids.astype(F32) - (iota(row_ids.shape, 1) // rank).astype(F32)


def expand_kernel(
    after, summands, ids, up, new_keys, keys_again, base_values, correction
):
    sources, all_rows, lanes = summands.shape
    adapters, rank, head_dim = up.shape
    rows = ids.shape[0]
    half = rows // 2
    tokens = all_rows - rank * rows // lanes
    add = lambda parts: sum((part.astype(F32) for part in parts[1:]), parts[0].astype(F32))
    fresh = add([summands[t, :tokens] for t in range(0, sources, 2)]).astype(BF16)
    new_keys[...] = fresh
    keys_again[...] = fresh
    base_values[...] = add([summands[t, :tokens] for t in range(1, sources, 2)])
    packed = add([summands[t, tokens:] for t in range(sources)]).T
    turned = pltpu.roll(packed, rank, 1)
    low = iota((half, LANES), 1) < rank
    shrunk = jnp.concatenate(
        [jnp.where(low, packed, turned), jnp.where(low, turned, packed)], axis=0
    )
    keys = lane_keys(ids[...], rank)
    per_vector = LANES // rank
    grown = jnp.zeros((rows, head_dim), F32)
    for first in range(0, adapters, per_vector):
        mine = jnp.where(keys == float(first), shrunk, 0.0).astype(BF16)
        block = up[first : first + per_vector].reshape(LANES, head_dim)
        grown = grown + jnp.dot(mine, block, preferred_element_type=F32)
    correction[...] = grown.astype(BF16)


def expand(after, summands, ids, up):
    sources, all_rows, lanes = summands.shape
    rows = ids.shape[0]
    _, rank, head_dim = up.shape
    tokens = all_rows - rank * rows // lanes
    return pl.pallas_call(
        expand_kernel,
        out_shape=(
            jax.ShapeDtypeStruct((tokens, head_dim), BF16),
            jax.ShapeDtypeStruct((tokens, head_dim), BF16),
            jax.ShapeDtypeStruct((tokens, head_dim), F32),
            jax.ShapeDtypeStruct((rows, head_dim), BF16),
        ),
        in_specs=[ANY] + [VMEM] * 3,
        out_specs=(VMEM,) * 4,
        compiler_params=params(),
        name="expand",
    )(after, summands, ids, up)


def weigh_kernel(q, new_keys, out, norms, slot_of_token, weights, mixed, chosen, *, scale):
    steps, requests, cols = q.shape
    tokens, head_dim = new_keys.shape
    slot_rows = chosen.shape[1]
    slots = jnp.concatenate([slot_of_token[...]] * (slot_rows // LANES), axis=1)
    token, place = iota((tokens, slot_rows), 0), iota((tokens, slot_rows), 1)
    found = (place // steps == slots) & (place % steps == token // requests)
    chosen[...] = jnp.where(found, 1.0, 0.0).astype(BF16)
    groups = cols // head_dim
    keys = new_keys[...]
    rows = groups * requests
    for s in range(steps):
        q_rows = jnp.concatenate(
            [q[s, :, g * head_dim : (g + 1) * head_dim] for g in range(groups)], axis=0
        )
        scores = contract_last(q_rows, keys) * scale
        row, token = iota((rows, tokens), 0), iota((rows, tokens), 1)
        seen = (token % requests == row % requests) & (token // requests <= s)
        scores = jnp.where(seen, scores, MASKED)
        part = slice(s * rows, (s + 1) * rows)
        cached_top = norms[part, :1]
        cached_sum = norms[part, LANES // 2 : LANES // 2 + 1]
        top = jnp.maximum(jnp.max(scores, axis=1, keepdims=True), cached_top)
        fresh = jnp.exp(scores - top)
        rescale = jnp.exp(cached_top - top)
        norm = 1.0 / (cached_sum * rescale + jnp.sum(fresh, axis=1, keepdims=True))
        weights[part, :] = (fresh * norm).astype(BF16)
        mixed[part, :] = out[part, :] * (rescale * norm)


def weigh(q, new_keys, out, norms, slot_of_token, slot_rows):
    rows, head_dim = out.shape
    tokens = new_keys.shape[0]
    kernel = lambda *refs: weigh_kernel(*refs, scale=1.0 / math.sqrt(head_dim))
    return pl.pallas_call(
        kernel,
        out_shape=(
            jax.ShapeDtypeStruct((rows, tokens), BF16),
            jax.ShapeDtypeStruct((rows, head_dim), F32),
            jax.ShapeDtypeStruct((tokens, slot_rows), BF16),
        ),
        in_specs=[VMEM] * 5,
        out_specs=(VMEM,) * 3,
        compiler_params=params(),
        cost_estimate=pl.CostEstimate(
            flops=4 * rows * tokens * head_dim,
            bytes_accessed=16 * rows * head_dim,
            transcendentals=rows * tokens,
        ),
        name="weigh",
    )(q, new_keys, out, norms, slot_of_token)


def finish_kernel(returned, chosen, base_values, weights, mixed, values_out, attention):
    steps, requests, cols = attention.shape
    tokens, head_dim = base_values.shape
    groups = cols // head_dim
    correction = jnp.dot(chosen[...], returned[...], preferred_element_type=F32)
    values = (base_values[...] + ADAPTER_SCALE * correction).astype(BF16)
    values_out[...] = values
    rows = groups * requests
    for s in range(steps):
        part = slice(s * rows, (s + 1) * rows)
        fresh = jnp.dot(weights[part, :], values, preferred_element_type=F32)
        result = (mixed[part, :] + fresh).astype(BF16)
        for g in range(groups):
            attention[s, :, g * head_dim : (g + 1) * head_dim] = result[
                g * requests : (g + 1) * requests
            ]


def finish(returned, chosen, base_values, weights, mixed, attention_shape):
    return pl.pallas_call(
        finish_kernel,
        out_shape=(
            jax.ShapeDtypeStruct(base_values.shape, BF16),
            jax.ShapeDtypeStruct(attention_shape, BF16),
        ),
        in_specs=[VMEM] * 5,
        out_specs=(VMEM,) * 2,
        compiler_params=params(),
        name="finish",
    )(returned, chosen, base_values, weights, mixed)


def per_device(
    normed_hidden_rows,
    queries,
    key_weight,
    value_weight,
    adapter_down,
    adapter_up,
    adapter_ids,
    owner_map,
    cache_keys,
    cache_values,
    cache_lengths,
):
    steps, requests, _ = normed_hidden_rows.shape
    owners = lax.axis_size("batch")
    tensor_size = lax.axis_size("tensor")
    exchange = lambda a, axis: lax.all_to_all(a, axis, split_axis=0, concat_axis=0, tiled=True)

    packed, slot_of_token = pack(
        adapter_ids, owner_map, normed_hidden_rows, adapter_down.shape[0], owners
    )
    received = exchange(packed, "batch")
    place = lax.axis_index("tensor")[None]
    kept, given = project(place, normed_hidden_rows, key_weight, value_weight, tensor_size)
    neighbours = [(i, i ^ 1) for i in range(tensor_size)]
    taken = lax.ppermute(given, "tensor", neighbours)
    summands, ids = shrink(received, adapter_down, pair(kept, taken))
    cached = cached_attention(cache_lengths, summands, queries, cache_keys, cache_values)
    summands = exchange(summands, "tensor")
    new_keys, fresh_keys, base_values, correction = expand(cached[0], summands, ids, adapter_up)
    returned = exchange(correction, "batch")
    weights, mixed, chosen = weigh(
        queries, fresh_keys, *cached, slot_of_token, correction.shape[0]
    )
    values, attention = finish(returned, chosen, base_values, weights, mixed, queries.shape)
    shape = (steps, requests, new_keys.shape[1])
    return (new_keys.reshape(shape), values.reshape(shape), attention)


def solution(mesh):
    placed = (
        P(None, "batch", "tensor"),
        P(None, "batch", "tensor"),
        P("tensor", None),
        P("tensor", None),
        P("batch", None, "tensor"),
        P("batch", None, "tensor"),
        P("batch"),
        P(),
        P("batch", "tensor", None, None),
        P("batch", "tensor", None, None),
        P("batch"),
    )
    return jax.shard_map(
        per_device,
        mesh=mesh,
        in_specs=placed,
        out_specs=(
            P(None, "batch", "tensor"),
            P(None, "batch", "tensor"),
            P(None, "batch", "tensor"),
        ),
        check_vma=False,
    )
```

```python
import math

import jax
import jax.numpy as jnp
from jax import lax
from jax.experimental import pallas as pl
from jax.experimental.pallas import tpu as pltpu
from jax.sharding import PartitionSpec as P

HEADS = 64
KV_HEADS = 8
CAP = 2

ADAPTER_SCALE = 0.5
MASKED = -1e30

F32 = jnp.float32
BF16 = jnp.bfloat16
LANES = 128
VMEM = pl.BlockSpec(memory_space=pltpu.VMEM)
HBM = pl.BlockSpec(memory_space=pltpu.HBM)
ANY = pl.BlockSpec(memory_space=pl.ANY)
SMEM = pl.BlockSpec(memory_space=pltpu.SMEM)


def params(mebibytes=16):
    return pltpu.CompilerParams(vmem_limit_bytes=mebibytes * 1024 * 1024)


def iota(shape, dim):
    return lax.broadcasted_iota(jnp.int32, shape, dim)


def contract_last(a, b):
    return lax.dot_general(a, b, (((1,), (1,)), ((), ())), preferred_element_type=F32)


def pack_kernel(
    ids_in, map_in, x_in, packed, slot_of_token, ids, owner_map, x, counts, sems, *, per_owner
):
    copies = [
        pltpu.make_async_copy(source, target, sems.at[i])
        for i, (source, target) in enumerate(((ids_in, ids), (map_in, owner_map), (x_in, x)))
    ]
    for copy in copies:
        copy.start()
    steps, requests, cols = x.shape
    tokens = steps * requests
    slot_rows = packed.shape[0]
    for o in range(counts.shape[0]):
        counts[o] = 0
    token = iota((tokens, LANES), 0) % requests
    column = iota((1, tokens), 1) % requests
    slot_sub = jnp.zeros((tokens, LANES), jnp.int32)
    row_sub = jnp.zeros((tokens, LANES), jnp.int32)
    slot_lane = jnp.zeros((1, tokens), jnp.int32)
    copies[0].wait()
    copies[1].wait()
    for r in range(requests):
        storage = owner_map[ids[r]]
        owner = storage // per_owner
        rank = counts[owner]
        counts[owner] = rank + 1
        slot = owner * CAP + rank
        slot_sub = jnp.where(token == r, slot, slot_sub)
        row_sub = jnp.where(token == r, storage - owner * per_owner, row_sub)
        slot_lane = jnp.where(column == r, slot, slot_lane)
    slot_of_token[...] = slot_sub
    place = iota((slot_rows, tokens), 0)
    source = iota((slot_rows, tokens), 1)
    chosen = (place // steps == slot_lane) & (place % steps == source // requests)
    chosen = jnp.where(chosen, 1.0, 0.0).astype(BF16)
    packed[:, cols:] = jnp.dot(
        chosen, row_sub.astype(F32).astype(BF16), preferred_element_type=F32
    ).astype(BF16)
    copies[2].wait()
    rows = x[...].reshape(tokens, cols)
    packed[:, :cols] = jnp.dot(chosen, rows, preferred_element_type=F32).astype(BF16)


def pack(adapter_ids, owner_map, x, per_owner, owners):
    steps, requests, cols = x.shape
    slot_rows = owners * CAP * steps
    return pl.pallas_call(
        lambda *refs: pack_kernel(*refs, per_owner=per_owner),
        out_shape=(
            jax.ShapeDtypeStruct((slot_rows, cols + LANES), BF16),
            jax.ShapeDtypeStruct((steps * requests, LANES), jnp.int32),
        ),
        in_specs=[HBM, HBM, HBM],
        out_specs=(VMEM, VMEM),
        scratch_shapes=[
            pltpu.SMEM(adapter_ids.shape, jnp.int32),
            pltpu.SMEM(owner_map.shape, jnp.int32),
            pltpu.VMEM(x.shape, BF16),
            pltpu.SMEM((owners,), jnp.int32),
            pltpu.SemaphoreType.DMA((3,)),
        ],
        compiler_params=params(60),
        name="pack",
    )(adapter_ids, owner_map, x)


def project_kernel(place, x_in, key_in, value_in, kept, given, x, key_weight, value_weight, sems):
    moves = ((x_in, x), (key_in, key_weight), (value_in, value_weight))
    copies = [
        pltpu.make_async_copy(source, target, sems.at[i])
        for i, (source, target) in enumerate(moves)
    ]
    for copy in copies:
        copy.start()
    heads, tokens, head_dim = kept.shape
    copies[0].wait()
    rows = x[...].reshape(tokens, x.shape[2])
    copies[1].wait()
    keys = jnp.dot(rows, key_weight[...], preferred_element_type=F32)
    copies[2].wait()
    values = jnp.dot(rows, value_weight[...], preferred_element_type=F32)
    even = place[0] % 2 == 0
    mine = jnp.where(even, keys, values).astype(BF16)
    other = jnp.where(even, values, keys).astype(BF16)
    for h in range(heads):
        kept[h] = mine[:, h * head_dim : (h + 1) * head_dim]
        given[h] = other[:, h * head_dim : (h + 1) * head_dim]


def project(place, x, key_weight, value_weight, heads):
    steps, requests, cols = x.shape
    tokens = steps * requests
    head_dim = key_weight.shape[1] // heads
    return pl.pallas_call(
        project_kernel,
        out_shape=(jax.ShapeDtypeStruct((heads, tokens, head_dim), BF16),) * 2,
        in_specs=[SMEM] + [HBM] * 3,
        out_specs=(VMEM,) * 2,
        scratch_shapes=[pltpu.VMEM(a.shape, BF16) for a in (x, key_weight, value_weight)]
        + [pltpu.SemaphoreType.DMA((3,))],
        compiler_params=params(60),
        cost_estimate=pl.CostEstimate(
            flops=4 * tokens * cols * heads * head_dim,
            bytes_accessed=4 * cols * heads * head_dim,
            transcendentals=0,
        ),
        name="project",
    )(place, x, key_weight, value_weight)


def pair_kernel(after, kept, taken, out):
    out[...] = (kept[...].astype(F32) + taken[...].astype(F32)).astype(BF16)


def pair(after, kept, taken):
    return pl.pallas_call(
        pair_kernel,
        out_shape=jax.ShapeDtypeStruct(kept.shape, BF16),
        in_specs=[ANY] + [VMEM] * 2,
        out_specs=VMEM,
        compiler_params=params(),
        name="pair",
    )(after, kept, taken)


def cached_kernel(
    lengths, after, q_in, cache_keys, cache_values, out, norms, done,
    q, keys, values, q_rows, scores, weights, sems, *, scale
):
    moves = ((q_in, q), (cache_keys, keys), (cache_values, values))
    copies = [
        pltpu.make_async_copy(source, target, sems.at[i])
        for i, (source, target) in enumerate(moves)
    ]
    for copy in copies:
        copy.start()
    steps, requests, cols = q.shape
    positions, head_dim = keys.shape[2], keys.shape[3]
    groups = cols // head_dim
    rows = steps * groups
    copies[0].wait()
    for s in range(steps):
        for g in range(groups):
            start = (s * groups + g) * requests
            q_rows[start : start + requests] = q[s, :, g * head_dim : (g + 1) * head_dim].astype(
                F32
            )
    copies[1].wait()
    position = iota((rows, positions), 1)
    low = iota((rows, LANES), 1) < LANES // 2
    for r in range(requests):
        mine = pl.ds(r, rows, stride=requests)
        product = contract_last(q_rows[mine, :].astype(BF16), keys[r, 0]) * scale
        scores[r] = jnp.where(position < lengths[r], product, MASKED)
    for r in range(requests):
        mine = pl.ds(r, rows, stride=requests)
        top = jnp.max(scores[r], axis=1, keepdims=True)
        exponent = jnp.exp(scores[r] - top)
        weights[r] = exponent.astype(BF16)
        norms[mine, :] = jnp.where(low, top, jnp.sum(exponent, axis=1, keepdims=True))
    copies[2].wait()
    for r in range(requests):
        mine = pl.ds(r, rows, stride=requests)
        out[mine, :] = jnp.dot(weights[r], values[r, 0], preferred_element_type=F32)
    done[...] = jnp.zeros_like(done)


def cached_attention(lengths, after, q, cache_keys, cache_values):
    steps, requests, cols = q.shape
    positions, head_dim = cache_keys.shape[2], cache_keys.shape[3]
    rows = steps * requests * (cols // head_dim)
    return pl.pallas_call(
        lambda *refs: cached_kernel(*refs, scale=1.0 / math.sqrt(head_dim)),
        out_shape=(
            jax.ShapeDtypeStruct((rows, LANES), F32),
            jax.ShapeDtypeStruct((rows, LANES), F32),
            jax.ShapeDtypeStruct((8, LANES), F32),
        ),
        in_specs=[SMEM, ANY] + [HBM] * 3,
        out_specs=(VMEM,) * 3,
        scratch_shapes=[pltpu.VMEM(a.shape, BF16) for a in (q, cache_keys, cache_values)]
        + [
            pltpu.VMEM((rows, head_dim), F32),
            pltpu.VMEM((requests, rows // requests, positions), F32),
            pltpu.VMEM((requests, rows // requests, positions), BF16),
            pltpu.SemaphoreType.DMA((3,)),
        ],
        compiler_params=params(60),
        cost_estimate=pl.CostEstimate(
            flops=4 * rows * positions * head_dim,
            bytes_accessed=4 * requests * positions * head_dim,
            transcendentals=rows * positions,
        ),
        name="cached",
    )(lengths, after, q, cache_keys, cache_values)


def shrink_kernel(received, down, partials, out, ids):
    adapters, rank, cols = down.shape
    rows = received.shape[0]
    per_part = 8
    ids[...] = received[:, cols:]
    wide = jnp.concatenate([ids[...].astype(F32)] * (rows // LANES), axis=1)
    diagonal = iota((rows, rows), 0) == iota((rows, rows), 1)
    adapter = jnp.sum(jnp.where(diagonal, wide, 0.0), axis=0, keepdims=True)
    partial = jnp.zeros((rank, rows), F32)
    for first in range(0, adapters, per_part):
        block = down[first : first + per_part].reshape(per_part * rank, cols)
        products = contract_last(block, received[:, :cols])
        for i in range(per_part):
            mine = adapter == float(first + i)
            partial = jnp.where(mine, products[i * rank : (i + 1) * rank], partial)
    partial = partial.astype(BF16)
    tokens = partials.shape[1]
    for t in range(out.shape[0]):
        out[t, :tokens] = partials[t]
        for i in range(rows // LANES):
            start = tokens + i * rank
            out[t, start : start + rank] = partial[:, i * LANES : (i + 1) * LANES]


def shrink(received, down, partials):
    adapters, rank, cols = down.shape
    rows = received.shape[0]
    heads, tokens, _ = partials.shape
    return pl.pallas_call(
        shrink_kernel,
        out_shape=(
            jax.ShapeDtypeStruct((heads, tokens + rank * rows // LANES, LANES), BF16),
            jax.ShapeDtypeStruct((rows, LANES), BF16),
        ),
        in_specs=[VMEM] * 3,
        out_specs=(VMEM,) * 2,
        compiler_params=params(),
        cost_estimate=pl.CostEstimate(
            flops=2 * rows * adapters * rank * cols,
            bytes_accessed=2 * adapters * rank * cols,
            transcendentals=0,
        ),
        name="shrink",
    )(received, down, partials)


def lane_keys(row_ids, rank):
    return row_ids.astype(F32) - (iota(row_ids.shape, 1) // rank).astype(F32)


def expand_kernel(
    summands, ids, up, new_keys, keys_again, base_values, correction
):
    sources, all_rows, lanes = summands.shape
    adapters, rank, head_dim = up.shape
    rows = ids.shape[0]
    half = rows // 2
    tokens = all_rows - rank * rows // lanes
    add = lambda parts: sum((part.astype(F32) for part in parts[1:]), parts[0].astype(F32))
    fresh = add([summands[t, :tokens] for t in range(0, sources, 2)]).astype(BF16)
    new_keys[...] = fresh
    keys_again[...] = fresh
    base_values[...] = add([summands[t, :tokens] for t in range(1, sources, 2)])
    packed = add([summands[t, tokens:] for t in range(sources)]).T
    turned = pltpu.roll(packed, rank, 1)
    low = iota((half, LANES), 1) < rank
    shrunk = jnp.concatenate(
        [jnp.where(low, packed, turned), jnp.where(low, turned, packed)], axis=0
    )
    keys = lane_keys(ids[...], rank)
    per_vector = LANES // rank
    grown = jnp.zeros((rows, head_dim), F32)
    for first in range(0, adapters, per_vector):
        mine = jnp.where(keys == float(first), shrunk, 0.0).astype(BF16)
        block = up[first : first + per_vector].reshape(LANES, head_dim)
        grown = grown + jnp.dot(mine, block, preferred_element_type=F32)
    correction[...] = grown.astype(BF16)


def expand(summands, ids, up):
    sources, all_rows, lanes = summands.shape
    rows = ids.shape[0]
    _, rank, head_dim = up.shape
    tokens = all_rows - rank * rows // lanes
    return pl.pallas_call(
        expand_kernel,
        out_shape=(
            jax.ShapeDtypeStruct((tokens, head_dim), BF16),
            jax.ShapeDtypeStruct((tokens, head_dim), BF16),
            jax.ShapeDtypeStruct((tokens, head_dim), F32),
            jax.ShapeDtypeStruct((rows, head_dim), BF16),
        ),
        in_specs=[VMEM] * 3,
        out_specs=(VMEM,) * 4,
        compiler_params=params(),
        name="expand",
    )(summands, ids, up)


def weigh_kernel(q, new_keys, out, norms, slot_of_token, weights, mixed, chosen, *, scale):
    steps, requests, cols = q.shape
    tokens, head_dim = new_keys.shape
    slot_rows = chosen.shape[1]
    slots = jnp.concatenate([slot_of_token[...]] * (slot_rows // LANES), axis=1)
    token, place = iota((tokens, slot_rows), 0), iota((tokens, slot_rows), 1)
    found = (place // steps == slots) & (place % steps == token // requests)
    chosen[...] = jnp.where(found, 1.0, 0.0).astype(BF16)
    groups = cols // head_dim
    keys = new_keys[...]
    rows = groups * requests
    for s in range(steps):
        q_rows = jnp.concatenate(
            [q[s, :, g * head_dim : (g + 1) * head_dim] for g in range(groups)], axis=0
        )
        scores = contract_last(q_rows, keys) * scale
        row, token = iota((rows, tokens), 0), iota((rows, tokens), 1)
        seen = (token % requests == row % requests) & (token // requests <= s)
        scores = jnp.where(seen, scores, MASKED)
        part = slice(s * rows, (s + 1) * rows)
        cached_top = norms[part, :1]
        cached_sum = norms[part, LANES // 2 : LANES // 2 + 1]
        top = jnp.maximum(jnp.max(scores, axis=1, keepdims=True), cached_top)
        fresh = jnp.exp(scores - top)
        rescale = jnp.exp(cached_top - top)
        norm = 1.0 / (cached_sum * rescale + jnp.sum(fresh, axis=1, keepdims=True))
        weights[part, :] = (fresh * norm).astype(BF16)
        mixed[part, :] = out[part, :] * (rescale * norm)


def weigh(q, new_keys, out, norms, slot_of_token, slot_rows):
    rows, head_dim = out.shape
    tokens = new_keys.shape[0]
    kernel = lambda *refs: weigh_kernel(*refs, scale=1.0 / math.sqrt(head_dim))
    return pl.pallas_call(
        kernel,
        out_shape=(
            jax.ShapeDtypeStruct((rows, tokens), BF16),
            jax.ShapeDtypeStruct((rows, head_dim), F32),
            jax.ShapeDtypeStruct((tokens, slot_rows), BF16),
        ),
        in_specs=[VMEM] * 5,
        out_specs=(VMEM,) * 3,
        compiler_params=params(),
        cost_estimate=pl.CostEstimate(
            flops=4 * rows * tokens * head_dim,
            bytes_accessed=16 * rows * head_dim,
            transcendentals=rows * tokens,
        ),
        name="weigh",
    )(q, new_keys, out, norms, slot_of_token)


def finish_kernel(returned, chosen, base_values, weights, mixed, values_out, attention):
    steps, requests, cols = attention.shape
    tokens, head_dim = base_values.shape
    groups = cols // head_dim
    correction = jnp.dot(chosen[...], returned[...], preferred_element_type=F32)
    values = (base_values[...] + ADAPTER_SCALE * correction).astype(BF16)
    values_out[...] = values
    rows = groups * requests
    for s in range(steps):
        part = slice(s * rows, (s + 1) * rows)
        fresh = jnp.dot(weights[part, :], values, preferred_element_type=F32)
        result = (mixed[part, :] + fresh).astype(BF16)
        for g in range(groups):
            attention[s, :, g * head_dim : (g + 1) * head_dim] = result[
                g * requests : (g + 1) * requests
            ]


def finish(returned, chosen, base_values, weights, mixed, attention_shape):
    return pl.pallas_call(
        finish_kernel,
        out_shape=(
            jax.ShapeDtypeStruct(base_values.shape, BF16),
            jax.ShapeDtypeStruct(attention_shape, BF16),
        ),
        in_specs=[VMEM] * 5,
        out_specs=(VMEM,) * 2,
        compiler_params=params(),
        name="finish",
    )(returned, chosen, base_values, weights, mixed)


def per_device(
    normed_hidden_rows,
    queries,
    key_weight,
    value_weight,
    adapter_down,
    adapter_up,
    adapter_ids,
    owner_map,
    cache_keys,
    cache_values,
    cache_lengths,
):
    steps, requests, _ = normed_hidden_rows.shape
    owners = lax.axis_size("batch")
    tensor_size = lax.axis_size("tensor")
    exchange = lambda a, axis: lax.all_to_all(a, axis, split_axis=0, concat_axis=0, tiled=True)

    packed, slot_of_token = pack(
        adapter_ids, owner_map, normed_hidden_rows, adapter_down.shape[0], owners
    )
    received = exchange(packed, "batch")
    place = lax.axis_index("tensor")[None]
    kept, given = project(place, normed_hidden_rows, key_weight, value_weight, tensor_size)
    neighbours = [(i, i ^ 1) for i in range(tensor_size)]
    taken = lax.ppermute(given, "tensor", neighbours)
    *cached, done = cached_attention(cache_lengths, given, queries, cache_keys, cache_values)
    summands, ids = shrink(received, adapter_down, pair(done, kept, taken))
    summands = exchange(summands, "tensor")
    new_keys, fresh_keys, base_values, correction = expand(summands, ids, adapter_up)
    returned = exchange(correction, "batch")
    weights, mixed, chosen = weigh(
        queries, fresh_keys, *cached, slot_of_token, correction.shape[0]
    )
    values, attention = finish(returned, chosen, base_values, weights, mixed, queries.shape)
    shape = (steps, requests, new_keys.shape[1])
    return (new_keys.reshape(shape), values.reshape(shape), attention)


def solution(mesh):
    placed = (
        P(None, "batch", "tensor"),
        P(None, "batch", "tensor"),
        P("tensor", None),
        P("tensor", None),
        P("batch", None, "tensor"),
        P("batch", None, "tensor"),
        P("batch"),
        P(),
        P("batch", "tensor", None, None),
        P("batch", "tensor", None, None),
        P("batch"),
    )
    return jax.shard_map(
        per_device,
        mesh=mesh,
        in_specs=placed,
        out_specs=(
            P(None, "batch", "tensor"),
            P(None, "batch", "tensor"),
            P(None, "batch", "tensor"),
        ),
        check_vma=False,
    )
```

```python
import math

import jax
import jax.numpy as jnp
from jax import lax
from jax.experimental import pallas as pl
from jax.experimental.pallas import tpu as pltpu
from jax.sharding import PartitionSpec as P

HEADS = 64
KV_HEADS = 8
CAP = 2

ADAPTER_SCALE = 0.5
MASKED = -1e30

F32 = jnp.float32
BF16 = jnp.bfloat16
LANES = 128
VMEM = pl.BlockSpec(memory_space=pltpu.VMEM)
HBM = pl.BlockSpec(memory_space=pltpu.HBM)
ANY = pl.BlockSpec(memory_space=pl.ANY)
SMEM = pl.BlockSpec(memory_space=pltpu.SMEM)


def params(mebibytes=16):
    return pltpu.CompilerParams(vmem_limit_bytes=mebibytes * 1024 * 1024)


def iota(shape, dim):
    return lax.broadcasted_iota(jnp.int32, shape, dim)


def contract_last(a, b):
    return lax.dot_general(a, b, (((1,), (1,)), ((), ())), preferred_element_type=F32)


def pack_kernel(
    ids_in, map_in, x_in, packed, slot_of_token, ids, owner_map, x, counts, sems, *, per_owner
):
    copies = [
        pltpu.make_async_copy(source, target, sems.at[i])
        for i, (source, target) in enumerate(((ids_in, ids), (map_in, owner_map), (x_in, x)))
    ]
    for copy in copies:
        copy.start()
    steps, requests, cols = x.shape
    tokens = steps * requests
    slot_rows = packed.shape[0]
    for o in range(counts.shape[0]):
        counts[o] = 0
    token = iota((tokens, LANES), 0) % requests
    column = iota((1, tokens), 1) % requests
    slot_sub = jnp.zeros((tokens, LANES), jnp.int32)
    row_sub = jnp.zeros((tokens, LANES), jnp.int32)
    slot_lane = jnp.zeros((1, tokens), jnp.int32)
    copies[0].wait()
    copies[1].wait()
    for r in range(requests):
        storage = owner_map[ids[r]]
        owner = storage // per_owner
        rank = counts[owner]
        counts[owner] = rank + 1
        slot = owner * CAP + rank
        slot_sub = jnp.where(token == r, slot, slot_sub)
        row_sub = jnp.where(token == r, storage - owner * per_owner, row_sub)
        slot_lane = jnp.where(column == r, slot, slot_lane)
    slot_of_token[...] = slot_sub
    place = iota((slot_rows, tokens), 0)
    source = iota((slot_rows, tokens), 1)
    chosen = (place // steps == slot_lane) & (place % steps == source // requests)
    chosen = jnp.where(chosen, 1.0, 0.0).astype(BF16)
    packed[:, cols:] = jnp.dot(
        chosen, row_sub.astype(F32).astype(BF16), preferred_element_type=F32
    ).astype(BF16)
    copies[2].wait()
    rows = x[...].reshape(tokens, cols)
    packed[:, :cols] = jnp.dot(chosen, rows, preferred_element_type=F32).astype(BF16)


def pack(adapter_ids, owner_map, x, per_owner, owners):
    steps, requests, cols = x.shape
    slot_rows = owners * CAP * steps
    return pl.pallas_call(
        lambda *refs: pack_kernel(*refs, per_owner=per_owner),
        out_shape=(
            jax.ShapeDtypeStruct((slot_rows, cols + LANES), BF16),
            jax.ShapeDtypeStruct((steps * requests, LANES), jnp.int32),
        ),
        in_specs=[HBM, HBM, HBM],
        out_specs=(VMEM, VMEM),
        scratch_shapes=[
            pltpu.SMEM(adapter_ids.shape, jnp.int32),
            pltpu.SMEM(owner_map.shape, jnp.int32),
            pltpu.VMEM(x.shape, BF16),
            pltpu.SMEM((owners,), jnp.int32),
            pltpu.SemaphoreType.DMA((3,)),
        ],
        compiler_params=params(60),
        name="pack",
    )(adapter_ids, owner_map, x)


def start_weight(wanted_keys, key_in, value_in, weight, sem):
    @pl.when(wanted_keys)
    def _():
        pltpu.make_async_copy(key_in, weight, sem).start()

    @pl.when(jnp.logical_not(wanted_keys))
    def _():
        pltpu.make_async_copy(value_in, weight, sem).start()

    return pltpu.make_async_copy(key_in, weight, sem)


def project(x, weight, out):
    heads, tokens, head_dim = out.shape
    rows = x[...].reshape(tokens, x.shape[2])
    product = jnp.dot(rows, weight[...], preferred_element_type=F32).astype(BF16)
    for h in range(heads):
        out[h] = product[:, h * head_dim : (h + 1) * head_dim]


def given_kernel(place, x_in, key_in, value_in, given, x, weight, sems):
    tokens_copy = pltpu.make_async_copy(x_in, x, sems.at[0])
    weight_copy = start_weight(place[0] % 2 == 1, key_in, value_in, weight, sems.at[1])
    tokens_copy.start()
    tokens_copy.wait()
    weight_copy.wait()
    project(x, weight, given)


def given_sums(place, x, key_weight, value_weight, heads):
    steps, requests, cols = x.shape
    tokens = steps * requests
    head_dim = key_weight.shape[1] // heads
    return pl.pallas_call(
        given_kernel,
        out_shape=jax.ShapeDtypeStruct((heads, tokens, head_dim), BF16),
        in_specs=[SMEM] + [HBM] * 3,
        out_specs=VMEM,
        scratch_shapes=[pltpu.VMEM(a.shape, BF16) for a in (x, key_weight)]
        + [pltpu.SemaphoreType.DMA((2,))],
        compiler_params=params(60),
        cost_estimate=pl.CostEstimate(
            flops=2 * tokens * cols * heads * head_dim,
            bytes_accessed=2 * cols * heads * head_dim,
            transcendentals=0,
        ),
        name="given",
    )(place, x, key_weight, value_weight)


def pair_kernel(kept, taken, out):
    out[...] = (kept[...].astype(F32) + taken[...].astype(F32)).astype(BF16)


def pair(kept, taken):
    return pl.pallas_call(
        pair_kernel,
        out_shape=jax.ShapeDtypeStruct(kept.shape, BF16),
        in_specs=[VMEM] * 2,
        out_specs=VMEM,
        compiler_params=params(),
        name="pair",
    )(kept, taken)


def cached_kernel(
    lengths, place, after, q_in, cache_keys, cache_values, x_in, key_in, value_in,
    kept, out, norms,
    q, keys, values, x, weight, q_rows, scores, weights, sems, *, scale
):
    moves = ((q_in, q), (cache_keys, keys), (x_in, x), (cache_values, values))
    copies = [
        pltpu.make_async_copy(source, target, sems.at[i])
        for i, (source, target) in enumerate(moves)
    ]
    for copy in copies[:3]:
        copy.start()
    weight_copy = start_weight(place[0] % 2 == 0, key_in, value_in, weight, sems.at[4])
    copies[3].start()
    steps, requests, cols = q.shape
    positions, head_dim = keys.shape[2], keys.shape[3]
    groups = cols // head_dim
    rows = steps * groups
    copies[0].wait()
    for s in range(steps):
        for g in range(groups):
            start = (s * groups + g) * requests
            q_rows[start : start + requests] = q[s, :, g * head_dim : (g + 1) * head_dim].astype(
                F32
            )
    copies[1].wait()
    position = iota((rows, positions), 1)
    low = iota((rows, LANES), 1) < LANES // 2
    for r in range(requests):
        mine = pl.ds(r, rows, stride=requests)
        product = contract_last(q_rows[mine, :].astype(BF16), keys[r, 0]) * scale
        scores[r] = jnp.where(position < lengths[r], product, MASKED)
    for r in range(requests):
        mine = pl.ds(r, rows, stride=requests)
        top = jnp.max(scores[r], axis=1, keepdims=True)
        exponent = jnp.exp(scores[r] - top)
        weights[r] = exponent.astype(BF16)
        norms[mine, :] = jnp.where(low, top, jnp.sum(exponent, axis=1, keepdims=True))
    copies[2].wait()
    weight_copy.wait()
    project(x, weight, kept)
    copies[3].wait()
    for r in range(requests):
        mine = pl.ds(r, rows, stride=requests)
        out[mine, :] = jnp.dot(weights[r], values[r, 0], preferred_element_type=F32)


def cached_attention(
    lengths, place, after, q, cache_keys, cache_values, x, key_weight, value_weight
):
    steps, requests, cols = q.shape
    positions, head_dim = cache_keys.shape[2], cache_keys.shape[3]
    rows = steps * requests * (cols // head_dim)
    return pl.pallas_call(
        lambda *refs: cached_kernel(*refs, scale=1.0 / math.sqrt(head_dim)),
        out_shape=(
            jax.ShapeDtypeStruct(after.shape, BF16),
            jax.ShapeDtypeStruct((rows, LANES), F32),
            jax.ShapeDtypeStruct((rows, LANES), F32),
        ),
        in_specs=[SMEM, SMEM, ANY] + [HBM] * 6,
        out_specs=(VMEM,) * 3,
        scratch_shapes=[
            pltpu.VMEM(a.shape, BF16) for a in (q, cache_keys, cache_values, x, key_weight)
        ]
        + [
            pltpu.VMEM((rows, head_dim), F32),
            pltpu.VMEM((requests, rows // requests, positions), F32),
            pltpu.VMEM((requests, rows // requests, positions), BF16),
            pltpu.SemaphoreType.DMA((5,)),
        ],
        compiler_params=params(60),
        cost_estimate=pl.CostEstimate(
            flops=4 * rows * positions * head_dim + 2 * x.size * key_weight.shape[1],
            bytes_accessed=4 * requests * positions * head_dim + 2 * key_weight.size,
            transcendentals=rows * positions,
        ),
        name="cached",
    )(lengths, place, after, q, cache_keys, cache_values, x, key_weight, value_weight)


def shrink_kernel(received, down, partials, out, ids):
    adapters, rank, cols = down.shape
    rows = received.shape[0]
    per_part = 8
    ids[...] = received[:, cols:]
    wide = jnp.concatenate([ids[...].astype(F32)] * (rows // LANES), axis=1)
    diagonal = iota((rows, rows), 0) == iota((rows, rows), 1)
    adapter = jnp.sum(jnp.where(diagonal, wide, 0.0), axis=0, keepdims=True)
    partial = jnp.zeros((rank, rows), F32)
    for first in range(0, adapters, per_part):
        block = down[first : first + per_part].reshape(per_part * rank, cols)
        products = contract_last(block, received[:, :cols])
        for i in range(per_part):
            mine = adapter == float(first + i)
            partial = jnp.where(mine, products[i * rank : (i + 1) * rank], partial)
    partial = partial.astype(BF16)
    tokens = partials.shape[1]
    for t in range(out.shape[0]):
        out[t, :tokens] = partials[t]
        for i in range(rows // LANES):
            start = tokens + i * rank
            out[t, start : start + rank] = partial[:, i * LANES : (i + 1) * LANES]


def shrink(received, down, partials):
    adapters, rank, cols = down.shape
    rows = received.shape[0]
    heads, tokens, _ = partials.shape
    return pl.pallas_call(
        shrink_kernel,
        out_shape=(
            jax.ShapeDtypeStruct((heads, tokens + rank * rows // LANES, LANES), BF16),
            jax.ShapeDtypeStruct((rows, LANES), BF16),
        ),
        in_specs=[VMEM] * 3,
        out_specs=(VMEM,) * 2,
        compiler_params=params(),
        cost_estimate=pl.CostEstimate(
            flops=2 * rows * adapters * rank * cols,
            bytes_accessed=2 * adapters * rank * cols,
            transcendentals=0,
        ),
        name="shrink",
    )(received, down, partials)


def lane_keys(row_ids, rank):
    return row_ids.astype(F32) - (iota(row_ids.shape, 1) // rank).astype(F32)


def expand_kernel(
    summands, ids, up, new_keys, keys_again, base_values, correction
):
    sources, all_rows, lanes = summands.shape
    adapters, rank, head_dim = up.shape
    rows = ids.shape[0]
    half = rows // 2
    tokens = all_rows - rank * rows // lanes
    add = lambda parts: sum((part.astype(F32) for part in parts[1:]), parts[0].astype(F32))
    fresh = add([summands[t, :tokens] for t in range(0, sources, 2)]).astype(BF16)
    new_keys[...] = fresh
    keys_again[...] = fresh
    base_values[...] = add([summands[t, :tokens] for t in range(1, sources, 2)])
    packed = add([summands[t, tokens:] for t in range(sources)]).T
    turned = pltpu.roll(packed, rank, 1)
    low = iota((half, LANES), 1) < rank
    shrunk = jnp.concatenate(
        [jnp.where(low, packed, turned), jnp.where(low, turned, packed)], axis=0
    )
    keys = lane_keys(ids[...], rank)
    per_vector = LANES // rank
    grown = jnp.zeros((rows, head_dim), F32)
    for first in range(0, adapters, per_vector):
        mine = jnp.where(keys == float(first), shrunk, 0.0).astype(BF16)
        block = up[first : first + per_vector].reshape(LANES, head_dim)
        grown = grown + jnp.dot(mine, block, preferred_element_type=F32)
    correction[...] = grown.astype(BF16)


def expand(summands, ids, up):
    sources, all_rows, lanes = summands.shape
    rows = ids.shape[0]
    _, rank, head_dim = up.shape
    tokens = all_rows - rank * rows // lanes
    return pl.pallas_call(
        expand_kernel,
        out_shape=(
            jax.ShapeDtypeStruct((tokens, head_dim), BF16),
            jax.ShapeDtypeStruct((tokens, head_dim), BF16),
            jax.ShapeDtypeStruct((tokens, head_dim), F32),
            jax.ShapeDtypeStruct((rows, head_dim), BF16),
        ),
        in_specs=[VMEM] * 3,
        out_specs=(VMEM,) * 4,
        compiler_params=params(),
        name="expand",
    )(summands, ids, up)


def weigh_kernel(q, new_keys, out, norms, slot_of_token, weights, mixed, chosen, *, scale):
    steps, requests, cols = q.shape
    tokens, head_dim = new_keys.shape
    slot_rows = chosen.shape[1]
    slots = jnp.concatenate([slot_of_token[...]] * (slot_rows // LANES), axis=1)
    token, place = iota((tokens, slot_rows), 0), iota((tokens, slot_rows), 1)
    found = (place // steps == slots) & (place % steps == token // requests)
    chosen[...] = jnp.where(found, 1.0, 0.0).astype(BF16)
    groups = cols // head_dim
    keys = new_keys[...]
    rows = groups * requests
    for s in range(steps):
        q_rows = jnp.concatenate(
            [q[s, :, g * head_dim : (g + 1) * head_dim] for g in range(groups)], axis=0
        )
        scores = contract_last(q_rows, keys) * scale
        row, token = iota((rows, tokens), 0), iota((rows, tokens), 1)
        seen = (token % requests == row % requests) & (token // requests <= s)
        scores = jnp.where(seen, scores, MASKED)
        part = slice(s * rows, (s + 1) * rows)
        cached_top = norms[part, :1]
        cached_sum = norms[part, LANES // 2 : LANES // 2 + 1]
        top = jnp.maximum(jnp.max(scores, axis=1, keepdims=True), cached_top)
        fresh = jnp.exp(scores - top)
        rescale = jnp.exp(cached_top - top)
        norm = 1.0 / (cached_sum * rescale + jnp.sum(fresh, axis=1, keepdims=True))
        weights[part, :] = (fresh * norm).astype(BF16)
        mixed[part, :] = out[part, :] * (rescale * norm)


def weigh(q, new_keys, out, norms, slot_of_token, slot_rows):
    rows, head_dim = out.shape
    tokens = new_keys.shape[0]
    kernel = lambda *refs: weigh_kernel(*refs, scale=1.0 / math.sqrt(head_dim))
    return pl.pallas_call(
        kernel,
        out_shape=(
            jax.ShapeDtypeStruct((rows, tokens), BF16),
            jax.ShapeDtypeStruct((rows, head_dim), F32),
            jax.ShapeDtypeStruct((tokens, slot_rows), BF16),
        ),
        in_specs=[VMEM] * 5,
        out_specs=(VMEM,) * 3,
        compiler_params=params(),
        cost_estimate=pl.CostEstimate(
            flops=4 * rows * tokens * head_dim,
            bytes_accessed=16 * rows * head_dim,
            transcendentals=rows * tokens,
        ),
        name="weigh",
    )(q, new_keys, out, norms, slot_of_token)


def finish_kernel(returned, chosen, base_values, weights, mixed, values_out, attention):
    steps, requests, cols = attention.shape
    tokens, head_dim = base_values.shape
    groups = cols // head_dim
    correction = jnp.dot(chosen[...], returned[...], preferred_element_type=F32)
    values = (base_values[...] + ADAPTER_SCALE * correction).astype(BF16)
    values_out[...] = values
    rows = groups * requests
    for s in range(steps):
        part = slice(s * rows, (s + 1) * rows)
        fresh = jnp.dot(weights[part, :], values, preferred_element_type=F32)
        result = (mixed[part, :] + fresh).astype(BF16)
        for g in range(groups):
            attention[s, :, g * head_dim : (g + 1) * head_dim] = result[
                g * requests : (g + 1) * requests
            ]


def finish(returned, chosen, base_values, weights, mixed, attention_shape):
    return pl.pallas_call(
        finish_kernel,
        out_shape=(
            jax.ShapeDtypeStruct(base_values.shape, BF16),
            jax.ShapeDtypeStruct(attention_shape, BF16),
        ),
        in_specs=[VMEM] * 5,
        out_specs=(VMEM,) * 2,
        compiler_params=params(),
        name="finish",
    )(returned, chosen, base_values, weights, mixed)


def per_device(
    normed_hidden_rows,
    queries,
    key_weight,
    value_weight,
    adapter_down,
    adapter_up,
    adapter_ids,
    owner_map,
    cache_keys,
    cache_values,
    cache_lengths,
):
    steps, requests, _ = normed_hidden_rows.shape
    owners = lax.axis_size("batch")
    tensor_size = lax.axis_size("tensor")
    exchange = lambda a, axis: lax.all_to_all(a, axis, split_axis=0, concat_axis=0, tiled=True)

    packed, slot_of_token = pack(
        adapter_ids, owner_map, normed_hidden_rows, adapter_down.shape[0], owners
    )
    received = exchange(packed, "batch")
    place = lax.axis_index("tensor")[None]
    given = given_sums(place, normed_hidden_rows, key_weight, value_weight, tensor_size)
    neighbours = [(i, i ^ 1) for i in range(tensor_size)]
    taken = lax.ppermute(given, "tensor", neighbours)
    kept, *cached = cached_attention(
        cache_lengths,
        place,
        given,
        queries,
        cache_keys,
        cache_values,
        normed_hidden_rows,
        key_weight,
        value_weight,
    )
    summands, ids = shrink(received, adapter_down, pair(kept, taken))
    summands = exchange(summands, "tensor")
    new_keys, fresh_keys, base_values, correction = expand(summands, ids, adapter_up)
    returned = exchange(correction, "batch")
    weights, mixed, chosen = weigh(
        queries, fresh_keys, *cached, slot_of_token, correction.shape[0]
    )
    values, attention = finish(returned, chosen, base_values, weights, mixed, queries.shape)
    shape = (steps, requests, new_keys.shape[1])
    return (new_keys.reshape(shape), values.reshape(shape), attention)


def solution(mesh):
    placed = (
        P(None, "batch", "tensor"),
        P(None, "batch", "tensor"),
        P("tensor", None),
        P("tensor", None),
        P("batch", None, "tensor"),
        P("batch", None, "tensor"),
        P("batch"),
        P(),
        P("batch", "tensor", None, None),
        P("batch", "tensor", None, None),
        P("batch"),
    )
    return jax.shard_map(
        per_device,
        mesh=mesh,
        in_specs=placed,
        out_specs=(
            P(None, "batch", "tensor"),
            P(None, "batch", "tensor"),
            P(None, "batch", "tensor"),
        ),
        check_vma=False,
    )
```

```python
import math

import jax
import jax.numpy as jnp
from jax import lax
from jax.experimental import pallas as pl
from jax.experimental.pallas import tpu as pltpu
from jax.sharding import PartitionSpec as P

HEADS = 64
KV_HEADS = 8
CAP = 2

ADAPTER_SCALE = 0.5
MASKED = -1e30

F32 = jnp.float32
BF16 = jnp.bfloat16
LANES = 128
VMEM = pl.BlockSpec(memory_space=pltpu.VMEM)
HBM = pl.BlockSpec(memory_space=pltpu.HBM)
ANY = pl.BlockSpec(memory_space=pl.ANY)
SMEM = pl.BlockSpec(memory_space=pltpu.SMEM)


def params(mebibytes=16):
    return pltpu.CompilerParams(vmem_limit_bytes=mebibytes * 1024 * 1024)


def iota(shape, dim):
    return lax.broadcasted_iota(jnp.int32, shape, dim)


def contract_last(a, b):
    return lax.dot_general(a, b, (((1,), (1,)), ((), ())), preferred_element_type=F32)


def pack_kernel(
    ids_in, map_in, x_in, packed, slot_of_token, ids, owner_map, x, counts, sems, *, per_owner
):
    copies = [
        pltpu.make_async_copy(source, target, sems.at[i])
        for i, (source, target) in enumerate(((ids_in, ids), (map_in, owner_map), (x_in, x)))
    ]
    for copy in copies:
        copy.start()
    steps, requests, cols = x.shape
    tokens = steps * requests
    slot_rows = packed.shape[0]
    for o in range(counts.shape[0]):
        counts[o] = 0
    token = iota((tokens, LANES), 0) % requests
    column = iota((1, tokens), 1) % requests
    slot_sub = jnp.zeros((tokens, LANES), jnp.int32)
    row_sub = jnp.zeros((tokens, LANES), jnp.int32)
    slot_lane = jnp.zeros((1, tokens), jnp.int32)
    copies[0].wait()
    copies[1].wait()
    for r in range(requests):
        storage = owner_map[ids[r]]
        owner = storage // per_owner
        rank = counts[owner]
        counts[owner] = rank + 1
        slot = (counts.shape[0] - 1 - owner) * CAP + rank
        slot_sub = jnp.where(token == r, slot, slot_sub)
        row_sub = jnp.where(token == r, storage - owner * per_owner, row_sub)
        slot_lane = jnp.where(column == r, slot, slot_lane)
    slot_of_token[...] = slot_sub
    place = iota((slot_rows, tokens), 0)
    source = iota((slot_rows, tokens), 1)
    chosen = (place // steps == slot_lane) & (place % steps == source // requests)
    chosen = jnp.where(chosen, 1.0, 0.0).astype(BF16)
    packed[:, cols:] = jnp.dot(
        chosen, row_sub.astype(F32).astype(BF16), preferred_element_type=F32
    ).astype(BF16)
    copies[2].wait()
    rows = x[...].reshape(tokens, cols)
    packed[:, :cols] = jnp.dot(chosen, rows, preferred_element_type=F32).astype(BF16)


def pack(adapter_ids, owner_map, x, per_owner, owners):
    steps, requests, cols = x.shape
    slot_rows = owners * CAP * steps
    return pl.pallas_call(
        lambda *refs: pack_kernel(*refs, per_owner=per_owner),
        out_shape=(
            jax.ShapeDtypeStruct((slot_rows, cols + LANES), BF16),
            jax.ShapeDtypeStruct((steps * requests, LANES), jnp.int32),
        ),
        in_specs=[HBM, HBM, HBM],
        out_specs=(VMEM, VMEM),
        scratch_shapes=[
            pltpu.SMEM(adapter_ids.shape, jnp.int32),
            pltpu.SMEM(owner_map.shape, jnp.int32),
            pltpu.VMEM(x.shape, BF16),
            pltpu.SMEM((owners,), jnp.int32),
            pltpu.SemaphoreType.DMA((3,)),
        ],
        compiler_params=params(60),
        name="pack",
    )(adapter_ids, owner_map, x)


def start_weight(wanted_keys, key_in, value_in, weight, sem):
    @pl.when(wanted_keys)
    def _():
        pltpu.make_async_copy(key_in, weight, sem).start()

    @pl.when(jnp.logical_not(wanted_keys))
    def _():
        pltpu.make_async_copy(value_in, weight, sem).start()

    return pltpu.make_async_copy(key_in, weight, sem)


def project(x, weight, out):
    heads, tokens, head_dim = out.shape
    rows = x[...].reshape(tokens, x.shape[2])
    product = jnp.dot(rows, weight[...], preferred_element_type=F32).astype(BF16)
    for h in range(heads):
        out[h] = product[:, h * head_dim : (h + 1) * head_dim]


def given_kernel(place, x_in, key_in, value_in, given, x, weight, sems):
    tokens_copy = pltpu.make_async_copy(x_in, x, sems.at[0])
    weight_copy = start_weight(place[0] % 2 == 1, key_in, value_in, weight, sems.at[1])
    tokens_copy.start()
    tokens_copy.wait()
    weight_copy.wait()
    project(x, weight, given)


def given_sums(place, x, key_weight, value_weight, heads):
    steps, requests, cols = x.shape
    tokens = steps * requests
    head_dim = key_weight.shape[1] // heads
    return pl.pallas_call(
        given_kernel,
        out_shape=jax.ShapeDtypeStruct((heads, tokens, head_dim), BF16),
        in_specs=[SMEM] + [HBM] * 3,
        out_specs=VMEM,
        scratch_shapes=[pltpu.VMEM(a.shape, BF16) for a in (x, key_weight)]
        + [pltpu.SemaphoreType.DMA((2,))],
        compiler_params=params(60),
        cost_estimate=pl.CostEstimate(
            flops=2 * tokens * cols * heads * head_dim,
            bytes_accessed=2 * cols * heads * head_dim,
            transcendentals=0,
        ),
        name="given",
    )(place, x, key_weight, value_weight)


def pair_kernel(kept, taken, out):
    out[...] = (kept[...].astype(F32) + taken[...].astype(F32)).astype(BF16)


def pair(kept, taken):
    return pl.pallas_call(
        pair_kernel,
        out_shape=jax.ShapeDtypeStruct(kept.shape, BF16),
        in_specs=[VMEM] * 2,
        out_specs=VMEM,
        compiler_params=params(),
        name="pair",
    )(kept, taken)


def cached_kernel(
    lengths, place, after, q_in, cache_keys, cache_values, x_in, key_in, value_in,
    kept, out, norms,
    q, keys, values, x, weight, q_rows, scores, weights, sems, *, scale
):
    moves = ((q_in, q), (cache_keys, keys), (x_in, x), (cache_values, values))
    copies = [
        pltpu.make_async_copy(source, target, sems.at[i])
        for i, (source, target) in enumerate(moves)
    ]
    for copy in copies[:3]:
        copy.start()
    weight_copy = start_weight(place[0] % 2 == 0, key_in, value_in, weight, sems.at[4])
    copies[3].start()
    steps, requests, cols = q.shape
    positions, head_dim = keys.shape[2], keys.shape[3]
    groups = cols // head_dim
    rows = steps * groups
    copies[0].wait()
    for s in range(steps):
        for g in range(groups):
            start = (s * groups + g) * requests
            q_rows[start : start + requests] = q[s, :, g * head_dim : (g + 1) * head_dim].astype(
                F32
            )
    copies[1].wait()
    position = iota((rows, positions), 1)
    low = iota((rows, LANES), 1) < LANES // 2
    for r in range(requests):
        mine = pl.ds(r, rows, stride=requests)
        product = contract_last(q_rows[mine, :].astype(BF16), keys[r, 0]) * scale
        scores[r] = jnp.where(position < lengths[r], product, MASKED)
    for r in range(requests):
        mine = pl.ds(r, rows, stride=requests)
        top = jnp.max(scores[r], axis=1, keepdims=True)
        exponent = jnp.exp(scores[r] - top)
        weights[r] = exponent.astype(BF16)
        norms[mine, :] = jnp.where(low, top, jnp.sum(exponent, axis=1, keepdims=True))
    copies[2].wait()
    weight_copy.wait()
    project(x, weight, kept)
    copies[3].wait()
    for r in range(requests):
        mine = pl.ds(r, rows, stride=requests)
        out[mine, :] = jnp.dot(weights[r], values[r, 0], preferred_element_type=F32)


def cached_attention(
    lengths, place, after, q, cache_keys, cache_values, x, key_weight, value_weight
):
    steps, requests, cols = q.shape
    positions, head_dim = cache_keys.shape[2], cache_keys.shape[3]
    rows = steps * requests * (cols // head_dim)
    return pl.pallas_call(
        lambda *refs: cached_kernel(*refs, scale=1.0 / math.sqrt(head_dim)),
        out_shape=(
            jax.ShapeDtypeStruct(after.shape, BF16),
            jax.ShapeDtypeStruct((rows, LANES), F32),
            jax.ShapeDtypeStruct((rows, LANES), F32),
        ),
        in_specs=[SMEM, SMEM, ANY] + [HBM] * 6,
        out_specs=(VMEM,) * 3,
        scratch_shapes=[
            pltpu.VMEM(a.shape, BF16) for a in (q, cache_keys, cache_values, x, key_weight)
        ]
        + [
            pltpu.VMEM((rows, head_dim), F32),
            pltpu.VMEM((requests, rows // requests, positions), F32),
            pltpu.VMEM((requests, rows // requests, positions), BF16),
            pltpu.SemaphoreType.DMA((5,)),
        ],
        compiler_params=params(60),
        cost_estimate=pl.CostEstimate(
            flops=4 * rows * positions * head_dim + 2 * x.size * key_weight.shape[1],
            bytes_accessed=4 * requests * positions * head_dim + 2 * key_weight.size,
            transcendentals=rows * positions,
        ),
        name="cached",
    )(lengths, place, after, q, cache_keys, cache_values, x, key_weight, value_weight)


def shrink_kernel(received, down, partials, out, ids, *, order):
    adapters, rank, cols = down.shape
    rows = received.shape[0]
    per_part = 8
    ids[...] = received[:, cols:]
    wide = jnp.concatenate([ids[...].astype(F32)] * (rows // LANES), axis=1)
    diagonal = iota((rows, rows), 0) == iota((rows, rows), 1)
    adapter = jnp.sum(jnp.where(diagonal, wide, 0.0), axis=0, keepdims=True)
    partial = jnp.zeros((rank, rows), F32)
    for first in range(0, adapters, per_part):
        block = down[first : first + per_part].reshape(per_part * rank, cols)
        products = contract_last(block, received[:, :cols])
        for i in range(per_part):
            mine = adapter == float(first + i)
            partial = jnp.where(mine, products[i * rank : (i + 1) * rank], partial)
    partial = partial.astype(BF16)
    tokens = partials.shape[1]
    for t, head in enumerate(order):
        out[t, :tokens] = partials[head]
        for i in range(rows // LANES):
            start = tokens + i * rank
            out[t, start : start + rank] = partial[:, i * LANES : (i + 1) * LANES]


def shrink(received, down, partials, order):
    adapters, rank, cols = down.shape
    rows = received.shape[0]
    heads, tokens, _ = partials.shape
    return pl.pallas_call(
        lambda *refs: shrink_kernel(*refs, order=order),
        out_shape=(
            jax.ShapeDtypeStruct((heads, tokens + rank * rows // LANES, LANES), BF16),
            jax.ShapeDtypeStruct((rows, LANES), BF16),
        ),
        in_specs=[VMEM] * 3,
        out_specs=(VMEM,) * 2,
        compiler_params=params(),
        cost_estimate=pl.CostEstimate(
            flops=2 * rows * adapters * rank * cols,
            bytes_accessed=2 * adapters * rank * cols,
            transcendentals=0,
        ),
        name="shrink",
    )(received, down, partials)


def lane_keys(row_ids, rank):
    return row_ids.astype(F32) - (iota(row_ids.shape, 1) // rank).astype(F32)


def expand_kernel(
    summands, ids, up, new_keys, keys_again, base_values, correction, *, order
):
    sources, all_rows, lanes = summands.shape
    adapters, rank, head_dim = up.shape
    rows = ids.shape[0]
    half = rows // 2
    tokens = all_rows - rank * rows // lanes
    add = lambda parts: sum((part.astype(F32) for part in parts[1:]), parts[0].astype(F32))
    fresh = add([summands[t, :tokens] for t in range(sources) if order[t] % 2 == 0]).astype(BF16)
    new_keys[...] = fresh
    keys_again[...] = fresh
    base_values[...] = add([summands[t, :tokens] for t in range(sources) if order[t] % 2 == 1])
    packed = add([summands[t, tokens:] for t in range(sources)]).T
    turned = pltpu.roll(packed, rank, 1)
    low = iota((half, LANES), 1) < rank
    shrunk = jnp.concatenate(
        [jnp.where(low, packed, turned), jnp.where(low, turned, packed)], axis=0
    )
    keys = lane_keys(ids[...], rank)
    per_vector = LANES // rank
    grown = jnp.zeros((rows, head_dim), F32)
    for first in range(0, adapters, per_vector):
        mine = jnp.where(keys == float(first), shrunk, 0.0).astype(BF16)
        block = up[first : first + per_vector].reshape(LANES, head_dim)
        grown = grown + jnp.dot(mine, block, preferred_element_type=F32)
    correction[...] = grown.astype(BF16)


def expand(summands, ids, up, order):
    sources, all_rows, lanes = summands.shape
    rows = ids.shape[0]
    _, rank, head_dim = up.shape
    tokens = all_rows - rank * rows // lanes
    return pl.pallas_call(
        lambda *refs: expand_kernel(*refs, order=order),
        out_shape=(
            jax.ShapeDtypeStruct((tokens, head_dim), BF16),
            jax.ShapeDtypeStruct((tokens, head_dim), BF16),
            jax.ShapeDtypeStruct((tokens, head_dim), F32),
            jax.ShapeDtypeStruct((rows, head_dim), BF16),
        ),
        in_specs=[VMEM] * 3,
        out_specs=(VMEM,) * 4,
        compiler_params=params(),
        name="expand",
    )(summands, ids, up)


def weigh_kernel(q, new_keys, out, norms, slot_of_token, weights, mixed, chosen, *, scale):
    steps, requests, cols = q.shape
    tokens, head_dim = new_keys.shape
    slot_rows = chosen.shape[1]
    slots = jnp.concatenate([slot_of_token[...]] * (slot_rows // LANES), axis=1)
    token, place = iota((tokens, slot_rows), 0), iota((tokens, slot_rows), 1)
    found = (place // steps == slots) & (place % steps == token // requests)
    chosen[...] = jnp.where(found, 1.0, 0.0).astype(BF16)
    groups = cols // head_dim
    keys = new_keys[...]
    rows = groups * requests
    for s in range(steps):
        q_rows = jnp.concatenate(
            [q[s, :, g * head_dim : (g + 1) * head_dim] for g in range(groups)], axis=0
        )
        scores = contract_last(q_rows, keys) * scale
        row, token = iota((rows, tokens), 0), iota((rows, tokens), 1)
        seen = (token % requests == row % requests) & (token // requests <= s)
        scores = jnp.where(seen, scores, MASKED)
        part = slice(s * rows, (s + 1) * rows)
        cached_top = norms[part, :1]
        cached_sum = norms[part, LANES // 2 : LANES // 2 + 1]
        top = jnp.maximum(jnp.max(scores, axis=1, keepdims=True), cached_top)
        fresh = jnp.exp(scores - top)
        rescale = jnp.exp(cached_top - top)
        norm = 1.0 / (cached_sum * rescale + jnp.sum(fresh, axis=1, keepdims=True))
        weights[part, :] = (fresh * norm).astype(BF16)
        mixed[part, :] = out[part, :] * (rescale * norm)


def weigh(q, new_keys, out, norms, slot_of_token, slot_rows):
    rows, head_dim = out.shape
    tokens = new_keys.shape[0]
    kernel = lambda *refs: weigh_kernel(*refs, scale=1.0 / math.sqrt(head_dim))
    return pl.pallas_call(
        kernel,
        out_shape=(
            jax.ShapeDtypeStruct((rows, tokens), BF16),
            jax.ShapeDtypeStruct((rows, head_dim), F32),
            jax.ShapeDtypeStruct((tokens, slot_rows), BF16),
        ),
        in_specs=[VMEM] * 5,
        out_specs=(VMEM,) * 3,
        compiler_params=params(),
        cost_estimate=pl.CostEstimate(
            flops=4 * rows * tokens * head_dim,
            bytes_accessed=16 * rows * head_dim,
            transcendentals=rows * tokens,
        ),
        name="weigh",
    )(q, new_keys, out, norms, slot_of_token)


def finish_kernel(returned, chosen, base_values, weights, mixed, values_out, attention):
    steps, requests, cols = attention.shape
    tokens, head_dim = base_values.shape
    groups = cols // head_dim
    correction = jnp.dot(chosen[...], returned[...], preferred_element_type=F32)
    values = (base_values[...] + ADAPTER_SCALE * correction).astype(BF16)
    values_out[...] = values
    rows = groups * requests
    for s in range(steps):
        part = slice(s * rows, (s + 1) * rows)
        fresh = jnp.dot(weights[part, :], values, preferred_element_type=F32)
        result = (mixed[part, :] + fresh).astype(BF16)
        for g in range(groups):
            attention[s, :, g * head_dim : (g + 1) * head_dim] = result[
                g * requests : (g + 1) * requests
            ]


def finish(returned, chosen, base_values, weights, mixed, attention_shape):
    return pl.pallas_call(
        finish_kernel,
        out_shape=(
            jax.ShapeDtypeStruct(base_values.shape, BF16),
            jax.ShapeDtypeStruct(attention_shape, BF16),
        ),
        in_specs=[VMEM] * 5,
        out_specs=(VMEM,) * 2,
        compiler_params=params(),
        name="finish",
    )(returned, chosen, base_values, weights, mixed)


def per_device(
    normed_hidden_rows,
    queries,
    key_weight,
    value_weight,
    adapter_down,
    adapter_up,
    adapter_ids,
    owner_map,
    cache_keys,
    cache_values,
    cache_lengths,
):
    steps, requests, _ = normed_hidden_rows.shape
    owners = lax.axis_size("batch")
    tensor_size = lax.axis_size("tensor")
    owner_order = list(range(owners))[::-1]
    tensor_order = list(range(tensor_size))[::-1]
    exchange = lambda a, axis, order: lax.all_to_all(
        a, axis, split_axis=0, concat_axis=0, axis_index_groups=[order], tiled=True
    )

    packed, slot_of_token = pack(
        adapter_ids, owner_map, normed_hidden_rows, adapter_down.shape[0], owners
    )
    received = exchange(packed, "batch", owner_order)
    place = lax.axis_index("tensor")[None]
    given = given_sums(place, normed_hidden_rows, key_weight, value_weight, tensor_size)
    neighbours = [(i, i ^ 1) for i in range(tensor_size)]
    taken = lax.ppermute(given, "tensor", neighbours)
    kept, *cached = cached_attention(
        cache_lengths,
        place,
        given,
        queries,
        cache_keys,
        cache_values,
        normed_hidden_rows,
        key_weight,
        value_weight,
    )
    summands, ids = shrink(received, adapter_down, pair(kept, taken), tensor_order)
    summands = exchange(summands, "tensor", tensor_order)
    new_keys, fresh_keys, base_values, correction = expand(summands, ids, adapter_up, tensor_order)
    returned = exchange(correction, "batch", owner_order)
    weights, mixed, chosen = weigh(
        queries, fresh_keys, *cached, slot_of_token, correction.shape[0]
    )
    values, attention = finish(returned, chosen, base_values, weights, mixed, queries.shape)
    shape = (steps, requests, new_keys.shape[1])
    return (new_keys.reshape(shape), values.reshape(shape), attention)


def solution(mesh):
    placed = (
        P(None, "batch", "tensor"),
        P(None, "batch", "tensor"),
        P("tensor", None),
        P("tensor", None),
        P("batch", None, "tensor"),
        P("batch", None, "tensor"),
        P("batch"),
        P(),
        P("batch", "tensor", None, None),
        P("batch", "tensor", None, None),
        P("batch"),
    )
    return jax.shard_map(
        per_device,
        mesh=mesh,
        in_specs=placed,
        out_specs=(
            P(None, "batch", "tensor"),
            P(None, "batch", "tensor"),
            P(None, "batch", "tensor"),
        ),
        check_vma=False,
    )
```

```python
import math

import jax
import jax.numpy as jnp
from jax import lax
from jax.experimental import pallas as pl
from jax.experimental.pallas import tpu as pltpu
from jax.sharding import PartitionSpec as P

HEADS = 64
KV_HEADS = 8
CAP = 2

ADAPTER_SCALE = 0.5
MASKED = -1e30

F32 = jnp.float32
BF16 = jnp.bfloat16
LANES = 128
VMEM = pl.BlockSpec(memory_space=pltpu.VMEM)
HBM = pl.BlockSpec(memory_space=pltpu.HBM)
ANY = pl.BlockSpec(memory_space=pl.ANY)
SMEM = pl.BlockSpec(memory_space=pltpu.SMEM)


def params(mebibytes=16):
    return pltpu.CompilerParams(vmem_limit_bytes=mebibytes * 1024 * 1024)


def iota(shape, dim):
    return lax.broadcasted_iota(jnp.int32, shape, dim)


def contract_last(a, b):
    return lax.dot_general(a, b, (((1,), (1,)), ((), ())), preferred_element_type=F32)


def pack_kernel(
    ids_in, map_in, x_in, packed, slot_of_token, ids, owner_map, x, counts, sems, *, per_owner
):
    copies = [
        pltpu.make_async_copy(source, target, sems.at[i])
        for i, (source, target) in enumerate(((ids_in, ids), (map_in, owner_map), (x_in, x)))
    ]
    for copy in copies:
        copy.start()
    steps, requests, cols = x.shape
    tokens = steps * requests
    slot_rows = packed.shape[0]
    for o in range(counts.shape[0]):
        counts[o] = 0
    token = iota((tokens, LANES), 0) % requests
    column = iota((1, tokens), 1) % requests
    slot_sub = jnp.zeros((tokens, LANES), jnp.int32)
    row_sub = jnp.zeros((tokens, LANES), jnp.int32)
    slot_lane = jnp.zeros((1, tokens), jnp.int32)
    copies[0].wait()
    copies[1].wait()
    for r in range(requests):
        storage = owner_map[ids[r]]
        owner = storage // per_owner
        rank = counts[owner]
        counts[owner] = rank + 1
        slot = (counts.shape[0] - 1 - owner) * CAP + rank
        slot_sub = jnp.where(token == r, slot, slot_sub)
        row_sub = jnp.where(token == r, storage - owner * per_owner, row_sub)
        slot_lane = jnp.where(column == r, slot, slot_lane)
    slot_of_token[...] = slot_sub
    place = iota((slot_rows, tokens), 0)
    source = iota((slot_rows, tokens), 1)
    chosen = (place // steps == slot_lane) & (place % steps == source // requests)
    chosen = jnp.where(chosen, 1.0, 0.0).astype(BF16)
    packed[:, cols:] = jnp.dot(
        chosen, row_sub.astype(F32).astype(BF16), preferred_element_type=F32
    ).astype(BF16)
    copies[2].wait()
    rows = x[...].reshape(tokens, cols)
    packed[:, :cols] = jnp.dot(chosen, rows, preferred_element_type=F32).astype(BF16)


def pack(adapter_ids, owner_map, x, per_owner, owners):
    steps, requests, cols = x.shape
    slot_rows = owners * CAP * steps
    return pl.pallas_call(
        lambda *refs: pack_kernel(*refs, per_owner=per_owner),
        out_shape=(
            jax.ShapeDtypeStruct((slot_rows, cols + LANES), BF16),
            jax.ShapeDtypeStruct((steps * requests, LANES), jnp.int32),
        ),
        in_specs=[HBM, HBM, HBM],
        out_specs=(VMEM, VMEM),
        scratch_shapes=[
            pltpu.SMEM(adapter_ids.shape, jnp.int32),
            pltpu.SMEM(owner_map.shape, jnp.int32),
            pltpu.VMEM(x.shape, BF16),
            pltpu.SMEM((owners,), jnp.int32),
            pltpu.SemaphoreType.DMA((3,)),
        ],
        compiler_params=params(60),
        name="pack",
    )(adapter_ids, owner_map, x)


def start_weight(wanted_keys, key_in, value_in, weight, sem):
    @pl.when(wanted_keys)
    def _():
        pltpu.make_async_copy(key_in, weight, sem).start()

    @pl.when(jnp.logical_not(wanted_keys))
    def _():
        pltpu.make_async_copy(value_in, weight, sem).start()

    return pltpu.make_async_copy(key_in, weight, sem)


def project(x, weight, out):
    heads, tokens, head_dim = out.shape
    rows = x[...].reshape(tokens, x.shape[2])
    product = jnp.dot(rows, weight[...], preferred_element_type=F32).astype(BF16)
    for h in range(heads):
        out[h] = product[:, h * head_dim : (h + 1) * head_dim]


def given_kernel(place, x_in, key_in, value_in, given, x, weight, sems):
    tokens_copy = pltpu.make_async_copy(x_in, x, sems.at[0])
    weight_copy = start_weight(place[0] % 2 == 1, key_in, value_in, weight, sems.at[1])
    tokens_copy.start()
    tokens_copy.wait()
    weight_copy.wait()
    project(x, weight, given)


def given_sums(place, x, key_weight, value_weight, heads):
    steps, requests, cols = x.shape
    tokens = steps * requests
    head_dim = key_weight.shape[1] // heads
    return pl.pallas_call(
        given_kernel,
        out_shape=jax.ShapeDtypeStruct((heads, tokens, head_dim), BF16),
        in_specs=[SMEM] + [HBM] * 3,
        out_specs=VMEM,
        scratch_shapes=[pltpu.VMEM(a.shape, BF16) for a in (x, key_weight)]
        + [pltpu.SemaphoreType.DMA((2,))],
        compiler_params=params(60),
        cost_estimate=pl.CostEstimate(
            flops=2 * tokens * cols * heads * head_dim,
            bytes_accessed=2 * cols * heads * head_dim,
            transcendentals=0,
        ),
        name="given",
    )(place, x, key_weight, value_weight)


def pair_kernel(kept, taken, out):
    out[...] = (kept[...].astype(F32) + taken[...].astype(F32)).astype(BF16)


def pair(kept, taken):
    return pl.pallas_call(
        pair_kernel,
        out_shape=jax.ShapeDtypeStruct(kept.shape, BF16),
        in_specs=[VMEM] * 2,
        out_specs=VMEM,
        compiler_params=params(),
        name="pair",
    )(kept, taken)


def cached_kernel(
    lengths, place, after, q_in, cache_keys, cache_values, x_in, key_in, value_in,
    kept, out, norms,
    q, keys, values, x, weight, q_rows, scores, weights, sems, *, scale
):
    moves = ((q_in, q), (cache_keys, keys), (x_in, x), (cache_values, values))
    copies = [
        pltpu.make_async_copy(source, target, sems.at[i])
        for i, (source, target) in enumerate(moves)
    ]
    for copy in copies[:3]:
        copy.start()
    weight_copy = start_weight(place[0] % 2 == 0, key_in, value_in, weight, sems.at[4])
    copies[3].start()
    steps, requests, cols = q.shape
    positions, head_dim = keys.shape[2], keys.shape[3]
    groups = cols // head_dim
    rows = steps * groups
    copies[0].wait()
    for s in range(steps):
        for g in range(groups):
            start = (s * groups + g) * requests
            q_rows[start : start + requests] = q[s, :, g * head_dim : (g + 1) * head_dim].astype(
                F32
            )
    copies[1].wait()
    position = iota((rows, positions), 1)
    low = iota((rows, LANES), 1) < LANES // 2
    for r in range(requests):
        mine = pl.ds(r, rows, stride=requests)
        product = contract_last(q_rows[mine, :].astype(BF16), keys[r, 0]) * scale
        scores[r] = jnp.where(position < lengths[r], product, MASKED)
    for r in range(requests):
        mine = pl.ds(r, rows, stride=requests)
        top = jnp.max(scores[r], axis=1, keepdims=True)
        exponent = jnp.exp(scores[r] - top)
        weights[r] = exponent.astype(BF16)
        norms[mine, :] = jnp.where(low, top, jnp.sum(exponent, axis=1, keepdims=True))
    copies[2].wait()
    weight_copy.wait()
    project(x, weight, kept)
    copies[3].wait()
    for r in range(requests):
        mine = pl.ds(r, rows, stride=requests)
        out[mine, :] = jnp.dot(weights[r], values[r, 0], preferred_element_type=F32)


def cached_attention(
    lengths, place, after, q, cache_keys, cache_values, x, key_weight, value_weight
):
    steps, requests, cols = q.shape
    positions, head_dim = cache_keys.shape[2], cache_keys.shape[3]
    rows = steps * requests * (cols // head_dim)
    return pl.pallas_call(
        lambda *refs: cached_kernel(*refs, scale=1.0 / math.sqrt(head_dim)),
        out_shape=(
            jax.ShapeDtypeStruct(after.shape, BF16),
            jax.ShapeDtypeStruct((rows, LANES), F32),
            jax.ShapeDtypeStruct((rows, LANES), F32),
        ),
        in_specs=[SMEM, SMEM, ANY] + [HBM] * 6,
        out_specs=(VMEM,) * 3,
        scratch_shapes=[
            pltpu.VMEM(a.shape, BF16) for a in (q, cache_keys, cache_values, x, key_weight)
        ]
        + [
            pltpu.VMEM((rows, head_dim), F32),
            pltpu.VMEM((requests, rows // requests, positions), F32),
            pltpu.VMEM((requests, rows // requests, positions), BF16),
            pltpu.SemaphoreType.DMA((5,)),
        ],
        compiler_params=params(52),
        cost_estimate=pl.CostEstimate(
            flops=4 * rows * positions * head_dim + 2 * x.size * key_weight.shape[1],
            bytes_accessed=4 * requests * positions * head_dim + 2 * key_weight.size,
            transcendentals=rows * positions,
        ),
        name="cached",
    )(lengths, place, after, q, cache_keys, cache_values, x, key_weight, value_weight)


def shrink_kernel(received, down, partials, out, ids, *, order):
    adapters, rank, cols = down.shape
    rows = received.shape[0]
    per_part = 8
    ids[...] = received[:, cols:]
    wide = jnp.concatenate([ids[...].astype(F32)] * (rows // LANES), axis=1)
    diagonal = iota((rows, rows), 0) == iota((rows, rows), 1)
    adapter = jnp.sum(jnp.where(diagonal, wide, 0.0), axis=0, keepdims=True)
    partial = jnp.zeros((rank, rows), F32)
    for first in range(0, adapters, per_part):
        block = down[first : first + per_part].reshape(per_part * rank, cols)
        products = contract_last(block, received[:, :cols])
        for i in range(per_part):
            mine = adapter == float(first + i)
            partial = jnp.where(mine, products[i * rank : (i + 1) * rank], partial)
    partial = partial.astype(BF16)
    tokens = partials.shape[1]
    for t, head in enumerate(order):
        out[t, :tokens] = partials[head]
        for i in range(rows // LANES):
            start = tokens + i * rank
            out[t, start : start + rank] = partial[:, i * LANES : (i + 1) * LANES]


def shrink(received, down, partials, order):
    adapters, rank, cols = down.shape
    rows = received.shape[0]
    heads, tokens, _ = partials.shape
    return pl.pallas_call(
        lambda *refs: shrink_kernel(*refs, order=order),
        out_shape=(
            jax.ShapeDtypeStruct((heads, tokens + rank * rows // LANES, LANES), BF16),
            jax.ShapeDtypeStruct((rows, LANES), BF16),
        ),
        in_specs=[VMEM] * 3,
        out_specs=(VMEM,) * 2,
        compiler_params=params(),
        cost_estimate=pl.CostEstimate(
            flops=2 * rows * adapters * rank * cols,
            bytes_accessed=2 * adapters * rank * cols,
            transcendentals=0,
        ),
        name="shrink",
    )(received, down, partials)


def lane_keys(row_ids, rank):
    return row_ids.astype(F32) - (iota(row_ids.shape, 1) // rank).astype(F32)


def expand_kernel(
    summands, ids, up, new_keys, keys_again, base_values, correction, *, order
):
    sources, all_rows, lanes = summands.shape
    adapters, rank, head_dim = up.shape
    rows = ids.shape[0]
    half = rows // 2
    tokens = all_rows - rank * rows // lanes
    add = lambda parts: sum((part.astype(F32) for part in parts[1:]), parts[0].astype(F32))
    fresh = add([summands[t, :tokens] for t in range(sources) if order[t] % 2 == 0]).astype(BF16)
    new_keys[...] = fresh
    keys_again[...] = fresh
    base_values[...] = add([summands[t, :tokens] for t in range(sources) if order[t] % 2 == 1])
    packed = add([summands[t, tokens:] for t in range(sources)]).T
    turned = pltpu.roll(packed, rank, 1)
    low = iota((half, LANES), 1) < rank
    shrunk = jnp.concatenate(
        [jnp.where(low, packed, turned), jnp.where(low, turned, packed)], axis=0
    )
    keys = lane_keys(ids[...], rank)
    per_vector = LANES // rank
    grown = jnp.zeros((rows, head_dim), F32)
    for first in range(0, adapters, per_vector):
        mine = jnp.where(keys == float(first), shrunk, 0.0).astype(BF16)
        block = up[first : first + per_vector].reshape(LANES, head_dim)
        grown = grown + jnp.dot(mine, block, preferred_element_type=F32)
    correction[...] = grown.astype(BF16)


def expand(summands, ids, up, order):
    sources, all_rows, lanes = summands.shape
    rows = ids.shape[0]
    _, rank, head_dim = up.shape
    tokens = all_rows - rank * rows // lanes
    return pl.pallas_call(
        lambda *refs: expand_kernel(*refs, order=order),
        out_shape=(
            jax.ShapeDtypeStruct((tokens, head_dim), BF16),
            jax.ShapeDtypeStruct((tokens, head_dim), BF16),
            jax.ShapeDtypeStruct((tokens, head_dim), F32),
            jax.ShapeDtypeStruct((rows, head_dim), BF16),
        ),
        in_specs=[VMEM] * 3,
        out_specs=(VMEM,) * 4,
        compiler_params=params(),
        name="expand",
    )(summands, ids, up)


def weigh_kernel(
    q, new_keys, base_values, out, norms, slot_of_token, spread, mixed, chosen, *, scale
):
    steps, requests, cols = q.shape
    tokens, head_dim = new_keys.shape
    slot_rows = chosen.shape[1]
    slots = jnp.concatenate([slot_of_token[...]] * (slot_rows // LANES), axis=1)
    token, place = iota((tokens, slot_rows), 0), iota((tokens, slot_rows), 1)
    found = (place // steps == slots) & (place % steps == token // requests)
    chosen[...] = jnp.where(found, 1.0, 0.0).astype(BF16)
    groups = cols // head_dim
    keys = new_keys[...]
    base = base_values[...].astype(BF16)
    rows = groups * requests
    for s in range(steps):
        q_rows = jnp.concatenate(
            [q[s, :, g * head_dim : (g + 1) * head_dim] for g in range(groups)], axis=0
        )
        scores = contract_last(q_rows, keys) * scale
        row, token = iota((rows, tokens), 0), iota((rows, tokens), 1)
        seen = (token % requests == row % requests) & (token // requests <= s)
        scores = jnp.where(seen, scores, MASKED)
        part = slice(s * rows, (s + 1) * rows)
        cached_top = norms[part, :1]
        cached_sum = norms[part, LANES // 2 : LANES // 2 + 1]
        top = jnp.maximum(jnp.max(scores, axis=1, keepdims=True), cached_top)
        fresh = jnp.exp(scores - top)
        rescale = jnp.exp(cached_top - top)
        norm = 1.0 / (cached_sum * rescale + jnp.sum(fresh, axis=1, keepdims=True))
        weights = (fresh * norm).astype(BF16)
        spread[part, :] = (
            ADAPTER_SCALE * jnp.dot(weights, chosen[...], preferred_element_type=F32)
        ).astype(BF16)
        mixed[part, :] = out[part, :] * (rescale * norm) + jnp.dot(
            weights, base, preferred_element_type=F32
        )


def weigh(q, new_keys, base_values, out, norms, slot_of_token, slot_rows):
    rows, head_dim = out.shape
    tokens = new_keys.shape[0]
    kernel = lambda *refs: weigh_kernel(*refs, scale=1.0 / math.sqrt(head_dim))
    return pl.pallas_call(
        kernel,
        out_shape=(
            jax.ShapeDtypeStruct((rows, slot_rows), BF16),
            jax.ShapeDtypeStruct((rows, head_dim), F32),
            jax.ShapeDtypeStruct((tokens, slot_rows), BF16),
        ),
        in_specs=[VMEM] * 6,
        out_specs=(VMEM,) * 3,
        compiler_params=params(),
        cost_estimate=pl.CostEstimate(
            flops=4 * rows * tokens * head_dim,
            bytes_accessed=16 * rows * head_dim,
            transcendentals=rows * tokens,
        ),
        name="weigh",
    )(q, new_keys, base_values, out, norms, slot_of_token)


def finish_kernel(returned, chosen, base_values, spread, mixed, values_out, attention):
    steps, requests, cols = attention.shape
    tokens, head_dim = base_values.shape
    groups = cols // head_dim
    correction = jnp.dot(chosen[...], returned[...], preferred_element_type=F32)
    values_out[...] = (base_values[...] + ADAPTER_SCALE * correction).astype(BF16)
    rows = groups * requests
    for s in range(steps):
        part = slice(s * rows, (s + 1) * rows)
        fresh = jnp.dot(spread[part, :], returned[...], preferred_element_type=F32)
        result = (mixed[part, :] + fresh).astype(BF16)
        for g in range(groups):
            attention[s, :, g * head_dim : (g + 1) * head_dim] = result[
                g * requests : (g + 1) * requests
            ]


def finish(returned, chosen, base_values, spread, mixed, attention_shape):
    return pl.pallas_call(
        finish_kernel,
        out_shape=(
            jax.ShapeDtypeStruct(base_values.shape, BF16),
            jax.ShapeDtypeStruct(attention_shape, BF16),
        ),
        in_specs=[VMEM] * 5,
        out_specs=(VMEM,) * 2,
        compiler_params=params(),
        name="finish",
    )(returned, chosen, base_values, spread, mixed)


def per_device(
    normed_hidden_rows,
    queries,
    key_weight,
    value_weight,
    adapter_down,
    adapter_up,
    adapter_ids,
    owner_map,
    cache_keys,
    cache_values,
    cache_lengths,
):
    steps, requests, _ = normed_hidden_rows.shape
    owners = lax.axis_size("batch")
    tensor_size = lax.axis_size("tensor")
    owner_order = list(range(owners))[::-1]
    tensor_order = list(range(tensor_size))[::-1]
    exchange = lambda a, axis, order: lax.all_to_all(
        a, axis, split_axis=0, concat_axis=0, axis_index_groups=[order], tiled=True
    )

    packed, slot_of_token = pack(
        adapter_ids, owner_map, normed_hidden_rows, adapter_down.shape[0], owners
    )
    received = exchange(packed, "batch", owner_order)
    place = lax.axis_index("tensor")[None]
    given = given_sums(place, normed_hidden_rows, key_weight, value_weight, tensor_size)
    neighbours = [(i, i ^ 1) for i in range(tensor_size)]
    taken = lax.ppermute(given, "tensor", neighbours)
    kept, *cached = cached_attention(
        cache_lengths,
        place,
        given,
        queries,
        cache_keys,
        cache_values,
        normed_hidden_rows,
        key_weight,
        value_weight,
    )
    summands, ids = shrink(received, adapter_down, pair(kept, taken), tensor_order)
    summands = exchange(summands, "tensor", tensor_order)
    new_keys, fresh_keys, base_values, correction = expand(summands, ids, adapter_up, tensor_order)
    returned = exchange(correction, "batch", owner_order)
    spread, mixed, chosen = weigh(
        queries, fresh_keys, base_values, *cached, slot_of_token, correction.shape[0]
    )
    values, attention = finish(returned, chosen, base_values, spread, mixed, queries.shape)
    shape = (steps, requests, new_keys.shape[1])
    return (new_keys.reshape(shape), values.reshape(shape), attention)


def solution(mesh):
    placed = (
        P(None, "batch", "tensor"),
        P(None, "batch", "tensor"),
        P("tensor", None),
        P("tensor", None),
        P("batch", None, "tensor"),
        P("batch", None, "tensor"),
        P("batch"),
        P(),
        P("batch", "tensor", None, None),
        P("batch", "tensor", None, None),
        P("batch"),
    )
    return jax.shard_map(
        per_device,
        mesh=mesh,
        in_specs=placed,
        out_specs=(
            P(None, "batch", "tensor"),
            P(None, "batch", "tensor"),
            P(None, "batch", "tensor"),
        ),
        check_vma=False,
    )
```
